32 devices in a mesh: row: 4 (over y, core), col: 8 (over z, x).
Axes of the slice: x: 2, y: 2, z: 4, core: 2. Of those that a mesh axis runs over, the one named last changes fastest.
Arguments:
- inverse_slab: bfloat16 [65536, 2048], P('row', 'col'), may hold values from -0.0234375 to 0.0234375
- cot_solved: bfloat16 [64, 65536], P(None, ('row', 'col')), may hold values from -6 to 6
- cot_direct: bfloat16 [64, 2048], P(None, 'col'), may hold values from -6 to 6
- solved_panel: bfloat16 [64, 65536], P(None, 'col'), may hold values from -1.078125 to 1.078125
Outputs:
- grad_factor: float32 [64, 2048], P(None, 'col')
- grad_operator: bfloat16 [2048, 65536], P('row', 'col')
The draws below stay inside these ranges and needn't reach their ends.
All inputs are finite; a program needn't handle non-finite values.
Results may differ from the reference program's by a relative error of at most 0.0049.
Values may be sent and summed in bfloat16 or wider, within the bound.
A program may use at most 64 MiB of HBM per device.

```python
import jax
import jax.numpy as jnp
from jax import lax

N = 65536
K = 64
W = 2048


def levels(stream_key, shape, pieces, low, top_value):
    gain = 1.0
    for axis_at, blocks in pieces:
        heights = jax.random.uniform(jax.random.fold_in(jax.random.fold_in(stream_key, 6), axis_at), (blocks,), jnp.float32, low / len(pieces), top_value / len(pieces))
        gain = gain * jnp.repeat(jnp.exp(heights), shape[axis_at] // blocks).reshape((-1,) + (1,) * (len(shape) - 1 - axis_at))
    return gain


def bell_draw(stream_key, shape, spread, bound, cuts=(), held_as=jnp.bfloat16):
    entries = jax.random.normal(stream_key, shape, jnp.float32) * spread
    if len(cuts) > 0:
        entries = levels(stream_key, shape, cuts, -0.22, 0.18) * entries
    return jnp.clip(entries, min=-bound, max=bound).astype(held_as)


def setup_inputs(seed: int = 0) -> dict:
    streams_of = jax.random.split(jax.random.key(seed), 5)
    inverse_slab = bell_draw(streams_of[0], (N, W), N ** -0.5, 0.0234375, ((0, 4), (1, 8)))
    cot_solved = bell_draw(streams_of[1], (K, N), 1.0, 6.0, ((1, 32),))
    cot_direct = bell_draw(streams_of[2], (K, W), 1.0, 6.0, ((1, 8),))
    solved_panel = bell_draw(streams_of[3], (K, N), 0.18, 1.078125, ((1, 8),))
    return dict(inverse_slab=inverse_slab, cot_solved=cot_solved, cot_direct=cot_direct, solved_panel=solved_panel)


def reference(inverse_slab, cot_solved, cot_direct, solved_panel):
    scale = 1.0 / jnp.sqrt(jnp.float32(2.0))
    pulled = jnp.dot(cot_solved, inverse_slab, preferred_element_type=jnp.float32)
    grad_factor = (cot_direct.astype(jnp.float32) + pulled) * scale
    pulled_low = pulled.astype(jnp.bfloat16)
    width = pulled_low.shape[1]
    block = min(width, 1024)
    blocks = pulled_low.reshape(pulled_low.shape[0], width // block, block).transpose(1, 0, 2)

    def one_block(piece):
        value = lax.dot_general(piece, solved_panel, (((0,), (0,)), ((), ())), preferred_element_type=jnp.float32)
        return (value * -scale).astype(jnp.bfloat16)
    grad_operator = lax.map(one_block, blocks).reshape(width, solved_panel.shape[1])
    return (grad_factor, grad_operator)
```

```python
import functools

import jax
import jax.numpy as jnp
from jax import lax
from jax.experimental import pallas as pl
from jax.experimental.pallas import tpu as pltpu
from jax.sharding import PartitionSpec as P

MESH = pl.DeviceIdType.MESH
PIECE = 16


def when(*conds):
    traced = None
    for cond in conds:
        if cond is not True:
            traced = cond if traced is None else jnp.logical_and(traced, cond)
    if traced is None:
        return lambda body: body()
    return pl.when(traced)


def pull_kernel(n_row, n_col, pieces, chunks,
                inverse_ref, cot_ref, needed_ref, pulled_ref,
                gathered, inverse, part, arrived, low,
                load_sem, own_sem, recv_sem, send_sem, sum_send, sum_recv,
                total_send, total_recv, low_send, low_recv):
    row, col = lax.axis_index("row"), lax.axis_index("col")
    line = n_col // 2
    z, x = col // 2, col % 2
    other = 1 - x
    factor = n_col // n_row
    depth = cot_ref.shape[1]
    rows = cot_ref.shape[0] // chunks
    balance = line >= 4

    def load_inverse(at, slot):
        span = pl.ds(pl.multiple_of(at * depth, depth), depth)
        return pltpu.make_async_copy(inverse_ref.at[span], inverse.at[span], load_sem.at[slot])

    own = pltpu.make_async_copy(cot_ref, gathered.at[col], own_sem)
    own.start()

    barrier = pltpu.get_barrier_semaphore()

    def greet(to_row, to_col):
        pl.semaphore_signal(barrier, inc=1, device_id=(to_row, to_col), device_id_type=MESH)

    has_down, has_up = z > 0, z < line - 1
    greet(row, z * 2 + other)
    pl.when(has_down)(lambda: greet(row, col - 2))
    pl.when(has_up)(lambda: greet(row, col + 2))
    for step in range(1, n_row):
        greet(lax.rem(row + step, n_row), col)

    for at in range(n_col):
        load_inverse(lax.rem(col + at, n_col), lax.rem(col + at, n_col)).start()
    own.wait()
    pl.semaphore_wait(barrier, n_row + has_down.astype(jnp.int32) + has_up.astype(jnp.int32))

    def move(block, chunk, stream, to_col):
        piece = gathered.at[block, pl.ds(chunk * rows, rows), :]
        return pltpu.make_async_remote_copy(
            src_ref=piece, dst_ref=piece,
            send_sem=send_sem.at[stream, block, chunk], recv_sem=recv_sem.at[block, chunk],
            device_id=(row, to_col), device_id_type=MESH)

    UP, DOWN, ACROSS = 0, 1, 2
    half = chunks // 2
    sends = []

    def send(stream, block, chunk, *conds):
        to_col = {UP: col + 2, DOWN: col - 2, ACROSS: z * 2 + other}[stream]
        when(*conds)(lambda: move(block, chunk, stream, to_col).start())
        sends.append((stream, block, chunk, to_col, conds))

    def receive(block, chunk, *conds):
        when(*conds)(lambda: move(block, chunk, ACROSS, z * 2 + other).wait_recv())

    def across_ok(at_z, of_z, chunk):
        if not balance:
            return ()
        conds = [
            jnp.logical_not(jnp.logical_and(at_z == 1, of_z == 0)),
            jnp.logical_not(jnp.logical_and(at_z == line - 2, of_z == line - 1)),
        ]
        if chunk >= half:
            conds.append(jnp.logical_not(jnp.logical_and(at_z == 0, of_z == 1)))
            conds.append(jnp.logical_not(jnp.logical_and(at_z == line - 1, of_z == line - 2)))
        return conds

    def multiply(block):
        load_inverse(block, block).wait()
        span = pl.ds(pl.multiple_of(block * depth, depth), depth)
        part[...] += jnp.dot(gathered[block], inverse[span, :], preferred_element_type=jnp.float32)

    def take(block, *conds):
        @when(*conds)
        def _():
            for chunk in range(chunks):
                receive(block, chunk)
            multiply(block)

    def finish_pair(step):
        below, above = z - 1 - step, z + 1 + step
        late = balance and step == 0
        take(below * 2 + other, below >= 0, z != line - 1 if late else True)
        take(above * 2 + other, above < line, z != 0 if late else True)

    for chunk in range(chunks):
        send(UP, col, chunk, has_up)
        send(DOWN, col, chunk, has_down)
        send(ACROSS, col, chunk)
    part[...] = jnp.zeros_like(part)
    multiply(col)

    for step in range(line - 1):
        below, above = z - 1 - step, z + 1 + step
        from_below, from_above = below >= 0, above < line
        below_col, above_col = below * 2 + x, above * 2 + x
        for chunk in range(chunks):
            receive(below_col, chunk, from_below)
            send(UP, below_col, chunk, from_below, has_up)
            send(ACROSS, below_col, chunk, from_below, *across_ok(z, below, chunk))
            receive(above_col, chunk, from_above)
            send(DOWN, above_col, chunk, from_above, has_down)
            send(ACROSS, above_col, chunk, from_above, *across_ok(z, above, chunk))
        if step == line - 2 and balance:
            for chunk in range(half, chunks):
                send(DOWN, z * 2 + other, chunk, z == 1)
                send(UP, z * 2 + other, chunk, z == line - 2)
        pl.when(from_below)(lambda: multiply(below_col))
        pl.when(from_above)(lambda: multiply(above_col))
        if step == 0:
            for chunk in range(chunks):
                receive(z * 2 + other, chunk)
                if balance:
                    send(UP, z * 2 + other, chunk, z == 0)
                    send(DOWN, z * 2 + other, chunk, z == line - 1)
            multiply(z * 2 + other)
        else:
            finish_pair(step - 1)
    finish_pair(line - 2)
    if balance:
        take(z * 2 + 2 + other, z == 0)
        take(z * 2 - 2 + other, z == line - 1)

    def sum_copy(piece, source):
        return pltpu.make_async_remote_copy(
            src_ref=part.at[pl.ds(piece * PIECE, PIECE), :], dst_ref=arrived.at[source],
            send_sem=sum_send.at[piece], recv_sem=sum_recv.at[source],
            device_id=(piece, col), device_id_type=MESH)

    for piece in range(pieces):
        pl.when(row != piece)(lambda: sum_copy(piece, row).start())

    def total_copy(piece, to_row):
        span = pl.ds(pl.multiple_of(piece * PIECE, PIECE), PIECE)
        return pltpu.make_async_remote_copy(
            src_ref=pulled_ref.at[span, :], dst_ref=pulled_ref.at[span, :],
            send_sem=total_send.at[to_row], recv_sem=total_recv.at[piece],
            device_id=(to_row, col), device_id_type=MESH)

    def low_copy(piece, slot, to_row, to_col):
        span = pl.ds(pl.multiple_of(piece * PIECE, PIECE), PIECE)
        return pltpu.make_async_remote_copy(
            src_ref=low, dst_ref=needed_ref.at[slot, span, :],
            send_sem=low_send.at[to_col], recv_sem=low_recv.at[slot, piece],
            device_id=(to_row, to_col), device_id_type=MESH)

    user, slot = col // factor, col % factor

    @pl.when(row < pieces)
    def _():
        span = pl.ds(pl.multiple_of(row * PIECE, PIECE), PIECE)
        for step in range(1, n_row):
            source = lax.rem(row + step, n_row)
            sum_copy(row, source).wait_recv()
        arrived[row] = part[span, :]
        total = arrived[0]
        for source in range(1, n_row):
            total = total + arrived[source]
        low[...] = total.astype(jnp.bfloat16)
        pulled_ref[span, :] = total
        for to_col in range(n_col):
            mine = jnp.logical_and(user == row, col == to_col)
            pl.when(jnp.logical_not(mine))(lambda: low_copy(row, slot, user, to_col).start())
        for step in range(1, n_row):
            total_copy(row, lax.rem(row + step, n_row)).start()

        @pl.when(user == row)
        def _():
            needed_ref[slot, span, :] = low[...]

    for piece in range(pieces):
        pl.when(row != piece)(lambda: total_copy(piece, row).wait_recv())
        for at in range(factor):
            mine = jnp.logical_and(row == piece, col == factor * row + at)
            pl.when(jnp.logical_not(mine))(lambda: low_copy(piece, at, row, col).wait_recv())

    for stream, block, chunk, to_col, conds in sends:
        when(*conds)(lambda: move(block, chunk, stream, to_col).wait_send())
    for piece in range(pieces):
        pl.when(row != piece)(lambda: sum_copy(piece, row).wait_send())

    @pl.when(row < pieces)
    def _():
        for to_col in range(n_col):
            mine = jnp.logical_and(user == row, col == to_col)
            pl.when(jnp.logical_not(mine))(lambda: low_copy(row, slot, user, to_col).wait_send())
        for step in range(1, n_row):
            total_copy(row, lax.rem(row + step, n_row)).wait_send()


def operator_kernel(needed_ref, panel_ref, direct_ref, pulled_ref, factor_ref, operator_ref):
    scale = 1.0 / jnp.sqrt(jnp.float32(2.0))

    @pl.when(pl.program_id(0) == 0)
    def _():
        factor_ref[...] = (direct_ref[...].astype(jnp.float32) + pulled_ref[...]) * scale

    width = needed_ref.shape[2]
    for at in range(needed_ref.shape[0]):
        product = lax.dot_general(
            needed_ref[at], panel_ref[...], (((0,), (0,)), ((), ())), preferred_element_type=jnp.float32)
        operator_ref[at * width:(at + 1) * width, :] = (product * -scale).astype(jnp.bfloat16)


def body(n_row, n_col, inverse_slab, cot_solved, cot_direct, solved_panel):
    n_states, width = inverse_slab.shape
    columns, depth = cot_solved.shape
    factor = n_col // n_row
    pieces = min(n_row, columns // PIECE)
    chunks = 4 if depth >= 1024 else 1
    any_space = pl.BlockSpec(memory_space=pl.ANY)
    vmem = pl.BlockSpec(memory_space=pltpu.VMEM)
    dma = pltpu.SemaphoreType.DMA
    needed, pulled = pl.pallas_call(
        functools.partial(pull_kernel, n_row, n_col, pieces, chunks),
        out_shape=(
            jax.ShapeDtypeStruct((factor, columns, width), jnp.bfloat16),
            jax.ShapeDtypeStruct((columns, width), jnp.float32),
        ),
        in_specs=[any_space, any_space],
        out_specs=(vmem, vmem),
        scratch_shapes=[
            pltpu.VMEM((n_col, columns, depth), jnp.bfloat16),
            pltpu.VMEM((n_states, width), jnp.bfloat16),
            pltpu.VMEM((columns, width), jnp.float32),
            pltpu.VMEM((n_row, PIECE, width), jnp.float32),
            pltpu.VMEM((PIECE, width), jnp.bfloat16),
            dma((n_col,)), dma, dma((n_col, chunks)), dma((3, n_col, chunks)),
            dma((pieces,)), dma((n_row,)),
            dma((n_row,)), dma((pieces,)), dma((n_col,)), dma((factor, pieces)),
        ],
        compiler_params=pltpu.CompilerParams(
            collective_id=0, has_side_effects=True, vmem_limit_bytes=48 * 2**20),
        cost_estimate=pl.CostEstimate(
            flops=2 * columns * n_states * width, bytes_accessed=2 * n_states * width, transcendentals=0),
        name="pull",
    )(inverse_slab, cot_solved)

    panel_width = solved_panel.shape[1]
    tile = min(panel_width, 1024)
    return pl.pallas_call(
        operator_kernel,
        grid=(panel_width // tile,),
        out_shape=(
            jax.ShapeDtypeStruct((columns, width), jnp.float32),
            jax.ShapeDtypeStruct((factor * width, panel_width), jnp.bfloat16),
        ),
        in_specs=[
            pl.BlockSpec((factor, columns, width), lambda i: (0, 0, 0)),
            pl.BlockSpec((columns, tile), lambda i: (0, i)),
            pl.BlockSpec((columns, width), lambda i: (0, 0)),
            pl.BlockSpec((columns, width), lambda i: (0, 0)),
        ],
        out_specs=(
            pl.BlockSpec((columns, width), lambda i: (0, 0)),
            pl.BlockSpec((factor * width, tile), lambda i: (0, i)),
        ),
        compiler_params=pltpu.CompilerParams(vmem_limit_bytes=32 * 2**20),
        cost_estimate=pl.CostEstimate(
            flops=2 * columns * factor * width * panel_width,
            bytes_accessed=2 * factor * width * panel_width, transcendentals=0),
        name="operator",
    )(needed, solved_panel, cot_direct, pulled)


def solution(mesh):
    n_row, n_col = mesh.shape["row"], mesh.shape["col"]
    in_specs = (P("row", "col"), P(None, ("row", "col")), P(None, "col"), P(None, "col"))
    out_specs = (P(None, "col"), P("row", "col"))
    return jax.shard_map(
        functools.partial(body, n_row, n_col),
        mesh=mesh, in_specs=in_specs, out_specs=out_specs, check_vma=False)
```

```python
import functools

import jax
import jax.numpy as jnp
from jax import lax
from jax.experimental import pallas as pl
from jax.experimental.pallas import tpu as pltpu
from jax.sharding import PartitionSpec as P

MESH = pl.DeviceIdType.MESH
PIECE = 16


def when(*conds):
    traced = None
    for cond in conds:
        if cond is not True:
            traced = cond if traced is None else jnp.logical_and(traced, cond)
    if traced is None:
        return lambda body: body()
    return pl.when(traced)


def pull_kernel(n_row, n_col, pieces, chunks,
                inverse_ref, cot_ref, needed_ref, pulled_ref,
                gathered, inverse, part, arrived, low,
                load_sem, own_sem, recv_sem, send_sem, sum_send, sum_recv,
                total_send, total_recv, low_send, low_recv):
    row, col = lax.axis_index("row"), lax.axis_index("col")
    line = n_col // 2
    z, x = col // 2, col % 2
    other = 1 - x
    pair = z * 2 + other
    factor = n_col // n_row
    depth = cot_ref.shape[1]
    span_of = depth // chunks
    balance = line >= 4
    half = chunks // 2
    window = min(2, chunks)
    ticks = (line - 1) * chunks
    has_down, has_up = z > 0, z < line - 1

    def load_inverse(block):
        span = pl.ds(pl.multiple_of(block * depth, depth), depth)
        return pltpu.make_async_copy(inverse_ref.at[span], inverse.at[span], load_sem.at[block])

    def load_own(chunk):
        return pltpu.make_async_copy(
            cot_ref.at[:, pl.ds(chunk * span_of, span_of)], gathered.at[col, chunk], own_sem.at[chunk])

    for chunk in range(chunks):
        load_own(chunk).start()

    barrier = pltpu.get_barrier_semaphore()

    def greet(to_row, to_col):
        pl.semaphore_signal(barrier, inc=1, device_id=(to_row, to_col), device_id_type=MESH)

    greet(row, pair)
    pl.when(has_down)(lambda: greet(row, col - 2))
    pl.when(has_up)(lambda: greet(row, col + 2))
    for step in range(1, n_row):
        greet(lax.rem(row + step, n_row), col)

    for at in range(n_col):
        load_inverse(lax.rem(col + at, n_col)).start()
    part[...] = jnp.zeros_like(part)
    for chunk in range(chunks):
        load_own(chunk).wait()
    pl.semaphore_wait(barrier, n_row + has_down.astype(jnp.int32) + has_up.astype(jnp.int32))

    UP, DOWN, ACROSS = 0, 1, 2
    target = {UP: col + 2, DOWN: col - 2, ACROSS: pair}

    def move(stream, block, chunk):
        piece = gathered.at[block, chunk]
        return pltpu.make_async_remote_copy(
            src_ref=piece, dst_ref=piece,
            send_sem=send_sem.at[stream, block, chunk], recv_sem=recv_sem.at[block, chunk],
            device_id=(row, target[stream]), device_id_type=MESH)

    def receive(block, chunk, *conds):
        when(*conds)(lambda: move(ACROSS, block, chunk).wait_recv())

    def multiply(block, chunk, *conds):
        @when(*conds)
        def _():
            if chunk == 0:
                load_inverse(block).wait()
            span = pl.ds(pl.multiple_of(block * depth + chunk * span_of, span_of), span_of)
            part[...] += jnp.dot(
                gathered[block, chunk], inverse[span, :], preferred_element_type=jnp.float32)

    def entry(stream, at):
        step, chunk = divmod(at, chunks)
        leaves, sign = (has_up, -1) if stream == UP else (has_down, 1)
        start, before_end = (0, line - 2) if stream == UP else (line - 1, 1)
        if step == 0:
            return col, chunk, (leaves,)
        if step == line - 1:
            if not balance or chunk + half >= chunks:
                return None
            return pair, chunk + half, (z == before_end,)
        source = z + sign * step
        inside = source >= 0 if stream == UP else source < line
        if step == 1 and balance:
            first = z == start
            return jnp.where(first, pair, source * 2 + x), chunk, (leaves, jnp.logical_or(first, inside))
        return source * 2 + x, chunk, (leaves, inside)

    open_sends = []

    def start(stream, block, chunk, *conds):
        when(*conds)(lambda: move(stream, block, chunk).start())

    def finish(stream, block, chunk, *conds):
        when(*conds)(lambda: move(stream, block, chunk).wait_send())

    def advance(stream, tick):
        new = entry(stream, tick + window)
        if new is None:
            return
        if tick >= 0:
            old = entry(stream, tick)
            finish(stream, old[0], old[1], *old[2])
            open_sends.remove((stream, tick))
        start(stream, new[0], new[1], *new[2])
        open_sends.append((stream, tick + window))

    across = []

    def start_across(block, chunk, *conds):
        start(ACROSS, block, chunk, *conds)
        across.append((block, chunk, conds))

    def across_ok(of_z, chunk):
        if not balance:
            return ()
        conds = [
            jnp.logical_not(jnp.logical_and(z == 1, of_z == 0)),
            jnp.logical_not(jnp.logical_and(z == line - 2, of_z == line - 1)),
        ]
        if chunk >= half:
            conds.append(jnp.logical_not(jnp.logical_and(z == 0, of_z == 1)))
            conds.append(jnp.logical_not(jnp.logical_and(z == line - 1, of_z == line - 2)))
        return conds

    def pass_across(step, chunk):
        below, above = z - 1 - step, z + 1 + step
        start_across(below * 2 + x, chunk, below >= 0, *across_ok(below, chunk))
        start_across(above * 2 + x, chunk, above < line, *across_ok(above, chunk))

    def take(block, chunk, *conds):
        receive(block, chunk, *conds)
        multiply(block, chunk, *conds)

    def take_pair(step, chunk):
        below, above = z - 1 - step, z + 1 + step
        late = balance and step == 0 and chunk >= half
        take(below * 2 + other, chunk, below >= 0, z != line - 1 if late else True)
        take(above * 2 + other, chunk, above < line, z != 0 if late else True)

    for chunk in range(window):
        advance(UP, chunk - window)
        advance(DOWN, chunk - window)
        start_across(col, chunk)
    for chunk in range(chunks):
        multiply(col, chunk)

    for tick in range(ticks):
        step, chunk = divmod(tick, chunks)
        below, above = z - 1 - step, z + 1 + step
        receive(below * 2 + x, chunk, below >= 0)
        advance(UP, tick)
        receive(above * 2 + x, chunk, above < line)
        advance(DOWN, tick)
        if tick + window < chunks:
            start_across(col, tick + window)
        if 0 <= tick - window < chunks:
            pass_across(0, tick - window)
        if step >= 1:
            pass_across(step, chunk)
        multiply(below * 2 + x, chunk, below >= 0)
        multiply(above * 2 + x, chunk, above < line)
        if step == 0:
            take(pair, chunk)
        if step >= 2:
            take_pair(step - 2, chunk)
    for tick in range(ticks, ticks + chunks - half - window):
        advance(UP, tick)
        advance(DOWN, tick)
    for step in range(max(line - 3, 0), line - 1):
        for chunk in range(chunks):
            take_pair(step, chunk)
            if step == line - 2 and balance and chunk >= half:
                take(2 + other, chunk, z == 0)
                take((line - 2) * 2 + other, chunk, z == line - 1)

    def sum_copy(piece, source):
        return pltpu.make_async_remote_copy(
            src_ref=part.at[pl.ds(piece * PIECE, PIECE), :], dst_ref=arrived.at[source],
            send_sem=sum_send.at[piece], recv_sem=sum_recv.at[source],
            device_id=(piece, col), device_id_type=MESH)

    for piece in range(pieces):
        pl.when(row != piece)(lambda: sum_copy(piece, row).start())

    def total_copy(piece, to_row):
        span = pl.ds(pl.multiple_of(piece * PIECE, PIECE), PIECE)
        return pltpu.make_async_remote_copy(
            src_ref=pulled_ref.at[span, :], dst_ref=pulled_ref.at[span, :],
            send_sem=total_send.at[to_row], recv_sem=total_recv.at[piece],
            device_id=(to_row, col), device_id_type=MESH)

    def low_copy(piece, slot, to_row, to_col):
        span = pl.ds(pl.multiple_of(piece * PIECE, PIECE), PIECE)
        return pltpu.make_async_remote_copy(
            src_ref=low, dst_ref=needed_ref.at[slot, span, :],
            send_sem=low_send.at[to_col], recv_sem=low_recv.at[slot, piece],
            device_id=(to_row, to_col), device_id_type=MESH)

    user, slot = col // factor, col % factor

    @pl.when(row < pieces)
    def _():
        span = pl.ds(pl.multiple_of(row * PIECE, PIECE), PIECE)
        for step in range(1, n_row):
            source = lax.rem(row + step, n_row)
            sum_copy(row, source).wait_recv()
        arrived[row] = part[span, :]
        total = arrived[0]
        for source in range(1, n_row):
            total = total + arrived[source]
        low[...] = total.astype(jnp.bfloat16)
        pulled_ref[span, :] = total
        for to_col in range(n_col):
            mine = jnp.logical_and(user == row, col == to_col)
            pl.when(jnp.logical_not(mine))(lambda: low_copy(row, slot, user, to_col).start())
        for step in range(1, n_row):
            total_copy(row, lax.rem(row + step, n_row)).start()

        @pl.when(user == row)
        def _():
            needed_ref[slot, span, :] = low[...]

    for piece in range(pieces):
        pl.when(row != piece)(lambda: total_copy(piece, row).wait_recv())
        for at in range(factor):
            mine = jnp.logical_and(row == piece, col == factor * row + at)
            pl.when(jnp.logical_not(mine))(lambda: low_copy(piece, at, row, col).wait_recv())

    for stream, at in open_sends:
        block, chunk, conds = entry(stream, at)
        finish(stream, block, chunk, *conds)
    for block, chunk, conds in across:
        finish(ACROSS, block, chunk, *conds)
    for piece in range(pieces):
        pl.when(row != piece)(lambda: sum_copy(piece, row).wait_send())

    @pl.when(row < pieces)
    def _():
        for to_col in range(n_col):
            mine = jnp.logical_and(user == row, col == to_col)
            pl.when(jnp.logical_not(mine))(lambda: low_copy(row, slot, user, to_col).wait_send())
        for step in range(1, n_row):
            total_copy(row, lax.rem(row + step, n_row)).wait_send()


def operator_kernel(tile, needed_ref, panel_ref, direct_ref, pulled_ref, factor_ref, operator_ref,
                    left, factor, result, factor_sem, result_sem):
    scale = 1.0 / jnp.sqrt(jnp.float32(2.0))
    width = needed_ref.shape[2]
    for at in range(needed_ref.shape[0]):
        left[at * width:(at + 1) * width, :] = needed_ref[at].T

    def store(at):
        span = pl.ds(at * tile, tile)
        return pltpu.make_async_copy(result.at[at], operator_ref.at[:, span], result_sem.at[at])

    tiles = panel_ref.shape[1] // tile
    for at in range(tiles):
        product = jnp.dot(
            left[...], panel_ref[:, at * tile:(at + 1) * tile], preferred_element_type=jnp.float32)
        result[at] = (product * -scale).astype(jnp.bfloat16)
        store(at).start()
        if at == 0:
            factor[...] = (direct_ref[...].astype(jnp.float32) + pulled_ref[...]) * scale
            out = pltpu.make_async_copy(factor, factor_ref, factor_sem)
            out.start()
    for at in range(tiles):
        store(at).wait()
    out.wait()


def body(n_row, n_col, inverse_slab, cot_solved, cot_direct, solved_panel):
    n_states, width = inverse_slab.shape
    columns, depth = cot_solved.shape
    factor = n_col // n_row
    pieces = min(n_row, columns // PIECE)
    chunks = 4 if depth >= 1024 else 1
    hbm = pl.BlockSpec(memory_space=pltpu.HBM)
    vmem = pl.BlockSpec(memory_space=pltpu.VMEM)
    dma = pltpu.SemaphoreType.DMA
    needed, pulled = pl.pallas_call(
        functools.partial(pull_kernel, n_row, n_col, pieces, chunks),
        out_shape=(
            jax.ShapeDtypeStruct((factor, columns, width), jnp.bfloat16),
            jax.ShapeDtypeStruct((columns, width), jnp.float32),
        ),
        in_specs=[hbm, hbm],
        out_specs=(vmem, vmem),
        scratch_shapes=[
            pltpu.VMEM((n_col, chunks, columns, depth // chunks), jnp.bfloat16),
            pltpu.VMEM((n_states, width), jnp.bfloat16),
            pltpu.VMEM((columns, width), jnp.float32),
            pltpu.VMEM((n_row, PIECE, width), jnp.float32),
            pltpu.VMEM((PIECE, width), jnp.bfloat16),
            dma((n_col,)), dma((chunks,)), dma((n_col, chunks)), dma((3, n_col, chunks)),
            dma((pieces,)), dma((n_row,)),
            dma((n_row,)), dma((pieces,)), dma((n_col,)), dma((factor, pieces)),
        ],
        compiler_params=pltpu.CompilerParams(
            collective_id=0, has_side_effects=True, vmem_limit_bytes=48 * 2**20),
        cost_estimate=pl.CostEstimate(
            flops=2 * columns * n_states * width, bytes_accessed=2 * n_states * width, transcendentals=0),
        name="pull",
    )(inverse_slab, cot_solved)

    panel_width = solved_panel.shape[1]
    tile = min(panel_width, 512)
    tiles = panel_width // tile
    return pl.pallas_call(
        functools.partial(operator_kernel, tile),
        out_shape=(
            jax.ShapeDtypeStruct((columns, width), jnp.float32),
            jax.ShapeDtypeStruct((factor * width, panel_width), jnp.bfloat16),
        ),
        in_specs=[vmem] * 4,
        out_specs=(hbm, hbm),
        scratch_shapes=[
            pltpu.VMEM((factor * width, columns), jnp.bfloat16),
            pltpu.VMEM((columns, width), jnp.float32),
            pltpu.VMEM((tiles, factor * width, tile), jnp.bfloat16),
            dma, dma((tiles,)),
        ],
        compiler_params=pltpu.CompilerParams(vmem_limit_bytes=32 * 2**20),
        cost_estimate=pl.CostEstimate(
            flops=2 * columns * factor * width * panel_width,
            bytes_accessed=2 * factor * width * panel_width, transcendentals=0),
        name="operator",
    )(needed, solved_panel, cot_direct, pulled)


def solution(mesh):
    n_row, n_col = mesh.shape["row"], mesh.shape["col"]
    in_specs = (P("row", "col"), P(None, ("row", "col")), P(None, "col"), P(None, "col"))
    out_specs = (P(None, "col"), P("row", "col"))
    return jax.shard_map(
        functools.partial(body, n_row, n_col),
        mesh=mesh, in_specs=in_specs, out_specs=out_specs, check_vma=False)
```

```python
import functools

import jax
import jax.numpy as jnp
from jax import lax
from jax.experimental import pallas as pl
from jax.experimental.pallas import tpu as pltpu
from jax.sharding import PartitionSpec as P

MESH = pl.DeviceIdType.MESH
PIECE = 16


def when(*conds):
    traced = None
    for cond in conds:
        if cond is not True:
            traced = cond if traced is None else jnp.logical_and(traced, cond)
    if traced is None:
        return lambda body: body()
    return pl.when(traced)


def pull_kernel(n_row, n_col, pieces, chunks,
                inverse_ref, cot_ref, needed_ref, pulled_ref,
                gathered, inverse, part, arrived, low,
                load_sem, own_sem, recv_sem, send_sem, sum_send, sum_recv,
                total_send, total_recv, low_send, low_recv):
    row, col = lax.axis_index("row"), lax.axis_index("col")
    line = n_col // 2
    z, x = col // 2, col % 2
    other = 1 - x
    pair = z * 2 + other
    factor = n_col // n_row
    depth = cot_ref.shape[1]
    span_of = depth // chunks
    balance = line >= 4
    half = chunks // 2
    has_down, has_up = z > 0, z < line - 1

    def load_inverse(block):
        span = pl.ds(pl.multiple_of(block * depth, depth), depth)
        return pltpu.make_async_copy(inverse_ref.at[span], inverse.at[span], load_sem.at[block])

    def load_own(chunk):
        return pltpu.make_async_copy(
            cot_ref.at[:, pl.ds(chunk * span_of, span_of)], gathered.at[col, chunk], own_sem.at[chunk])

    for chunk in range(chunks):
        load_own(chunk).start()

    barrier = pltpu.get_barrier_semaphore()

    def greet(to_row, to_col):
        pl.semaphore_signal(barrier, inc=1, device_id=(to_row, to_col), device_id_type=MESH)

    greet(row, pair)
    pl.when(has_down)(lambda: greet(row, col - 2))
    pl.when(has_up)(lambda: greet(row, col + 2))
    for step in range(1, n_row):
        greet(lax.rem(row + step, n_row), col)

    for at in range(n_col):
        load_inverse(lax.rem(col + at, n_col)).start()
    part[...] = jnp.zeros_like(part)
    for chunk in range(chunks):
        load_own(chunk).wait()
    pl.semaphore_wait(barrier, n_row + has_down.astype(jnp.int32) + has_up.astype(jnp.int32))

    UP, DOWN, ACROSS = 0, 1, 2
    target = {UP: col + 2, DOWN: col - 2, ACROSS: pair}

    def move(stream, block, chunk):
        piece = gathered.at[block, chunk]
        return pltpu.make_async_remote_copy(
            src_ref=piece, dst_ref=piece,
            send_sem=send_sem.at[stream, block, chunk], recv_sem=recv_sem.at[block, chunk],
            device_id=(row, target[stream]), device_id_type=MESH)

    def receive(block, chunk, *conds):
        when(*conds)(lambda: move(ACROSS, block, chunk).wait_recv())

    def multiply(block):
        load_inverse(block).wait()
        total = part[...]
        for chunk in range(chunks):
            span = pl.ds(pl.multiple_of(block * depth + chunk * span_of, span_of), span_of)
            total += jnp.dot(
                gathered[block, chunk], inverse[span, :], preferred_element_type=jnp.float32)
        part[...] = total

    sends = []

    def send(stream, block, chunk, *conds):
        when(*conds)(lambda: move(stream, block, chunk).start())
        sends.append((stream, block, chunk, conds))

    def across_ok(of_z, chunk):
        if not balance:
            return ()
        if chunk >= half:
            return of_z != 0, of_z != line - 1
        return (jnp.logical_not(jnp.logical_and(z == 1, of_z == 0)),
                jnp.logical_not(jnp.logical_and(z == line - 2, of_z == line - 1)))

    def take_pair(step):
        for at, there in ((z - 1 - step, z - 1 - step >= 0), (z + 1 + step, z + 1 + step < line)):
            block = at * 2 + other

            @pl.when(there)
            def _():
                for chunk in range(chunks):
                    if balance and chunk >= half:
                        passed_on = jnp.logical_and(
                            jnp.logical_or(at == 0, at == line - 1), jnp.logical_and(has_up, has_down))
                        receive(block, chunk, jnp.logical_not(passed_on))
                    else:
                        receive(block, chunk)
                multiply(block)

    bottom, top = other, (line - 1) * 2 + other

    for chunk in range(chunks):
        send(UP, col, chunk, has_up)
        send(DOWN, col, chunk, has_down)
        send(ACROSS, col, chunk)
    multiply(col)

    for step in range(line - 1):
        below, above = z - 1 - step, z + 1 + step
        for chunk in range(chunks):
            receive(below * 2 + x, chunk, below >= 0)
            send(UP, below * 2 + x, chunk, below >= 0, has_up)
            send(ACROSS, below * 2 + x, chunk, below >= 0, *across_ok(below, chunk))
            receive(above * 2 + x, chunk, above < line)
            send(DOWN, above * 2 + x, chunk, above < line, has_down)
            send(ACROSS, above * 2 + x, chunk, above < line, *across_ok(above, chunk))
        if balance and step >= 1:
            for chunk in range(half, chunks):
                receive(bottom, chunk, z == step)
                send(UP, bottom, chunk, z == step)
                receive(top, chunk, z == line - 1 - step)
                send(DOWN, top, chunk, z == line - 1 - step)
        pl.when(below >= 0)(lambda: multiply(below * 2 + x))
        pl.when(above < line)(lambda: multiply(above * 2 + x))
        if step == 0:
            for chunk in range(chunks):
                receive(pair, chunk)
                if balance:
                    send(UP, pair, chunk, z == 0)
                    send(DOWN, pair, chunk, z == line - 1)
            multiply(pair)
        else:
            take_pair(step - 1)
    take_pair(line - 2)

    def sum_copy(piece, source):
        return pltpu.make_async_remote_copy(
            src_ref=part.at[pl.ds(piece * PIECE, PIECE), :], dst_ref=arrived.at[source],
            send_sem=sum_send.at[piece], recv_sem=sum_recv.at[source],
            device_id=(piece, col), device_id_type=MESH)

    for piece in range(pieces):
        pl.when(row != piece)(lambda: sum_copy(piece, row).start())

    def total_copy(piece, to_row):
        span = pl.ds(pl.multiple_of(piece * PIECE, PIECE), PIECE)
        return pltpu.make_async_remote_copy(
            src_ref=pulled_ref.at[span, :], dst_ref=pulled_ref.at[span, :],
            send_sem=total_send.at[to_row], recv_sem=total_recv.at[piece],
            device_id=(to_row, col), device_id_type=MESH)

    def low_copy(piece, slot, to_row, to_col):
        span = pl.ds(pl.multiple_of(piece * PIECE, PIECE), PIECE)
        return pltpu.make_async_remote_copy(
            src_ref=low, dst_ref=needed_ref.at[slot, span, :],
            send_sem=low_send.at[to_col], recv_sem=low_recv.at[slot, piece],
            device_id=(to_row, to_col), device_id_type=MESH)

    user, slot = col // factor, col % factor

    @pl.when(row < pieces)
    def _():
        span = pl.ds(pl.multiple_of(row * PIECE, PIECE), PIECE)
        for step in range(1, n_row):
            source = lax.rem(row + step, n_row)
            sum_copy(row, source).wait_recv()
        arrived[row] = part[span, :]
        total = arrived[0]
        for source in range(1, n_row):
            total = total + arrived[source]
        low[...] = total.astype(jnp.bfloat16)
        pulled_ref[span, :] = total
        for to_col in range(n_col):
            mine = jnp.logical_and(user == row, col == to_col)
            pl.when(jnp.logical_not(mine))(lambda: low_copy(row, slot, user, to_col).start())
        for step in range(1, n_row):
            total_copy(row, lax.rem(row + step, n_row)).start()

        @pl.when(user == row)
        def _():
            needed_ref[slot, span, :] = low[...]

    for piece in range(pieces):
        pl.when(row != piece)(lambda: total_copy(piece, row).wait_recv())
        for at in range(factor):
            mine = jnp.logical_and(row == piece, col == factor * row + at)
            pl.when(jnp.logical_not(mine))(lambda: low_copy(piece, at, row, col).wait_recv())

    for stream, block, chunk, conds in sends:
        when(*conds)(lambda: move(stream, block, chunk).wait_send())
    for piece in range(pieces):
        pl.when(row != piece)(lambda: sum_copy(piece, row).wait_send())

    @pl.when(row < pieces)
    def _():
        for to_col in range(n_col):
            mine = jnp.logical_and(user == row, col == to_col)
            pl.when(jnp.logical_not(mine))(lambda: low_copy(row, slot, user, to_col).wait_send())
        for step in range(1, n_row):
            total_copy(row, lax.rem(row + step, n_row)).wait_send()


def operator_kernel(tile, needed_ref, panel_ref, direct_ref, pulled_ref, factor_ref, operator_ref,
                    left, factor, result, factor_sem, result_sem):
    scale = 1.0 / jnp.sqrt(jnp.float32(2.0))
    width = needed_ref.shape[2]
    for at in range(needed_ref.shape[0]):
        left[at * width:(at + 1) * width, :] = needed_ref[at].T

    def store(at):
        span = pl.ds(at * tile, tile)
        return pltpu.make_async_copy(result.at[at], operator_ref.at[:, span], result_sem.at[at])

    tiles = panel_ref.shape[1] // tile
    for at in range(tiles):
        product = jnp.dot(
            left[...], panel_ref[:, at * tile:(at + 1) * tile], preferred_element_type=jnp.float32)
        result[at] = (product * -scale).astype(jnp.bfloat16)
        store(at).start()
        if at == 0:
            factor[...] = (direct_ref[...].astype(jnp.float32) + pulled_ref[...]) * scale
            out = pltpu.make_async_copy(factor, factor_ref, factor_sem)
            out.start()
    for at in range(tiles):
        store(at).wait()
    out.wait()


def body(n_row, n_col, inverse_slab, cot_solved, cot_direct, solved_panel):
    n_states, width = inverse_slab.shape
    columns, depth = cot_solved.shape
    factor = n_col // n_row
    pieces = min(n_row, columns // PIECE)
    chunks = 4 if depth >= 1024 else 1
    hbm = pl.BlockSpec(memory_space=pltpu.HBM)
    vmem = pl.BlockSpec(memory_space=pltpu.VMEM)
    dma = pltpu.SemaphoreType.DMA
    needed, pulled = pl.pallas_call(
        functools.partial(pull_kernel, n_row, n_col, pieces, chunks),
        out_shape=(
            jax.ShapeDtypeStruct((factor, columns, width), jnp.bfloat16),
            jax.ShapeDtypeStruct((columns, width), jnp.float32),
        ),
        in_specs=[hbm, hbm],
        out_specs=(vmem, vmem),
        scratch_shapes=[
            pltpu.VMEM((n_col, chunks, columns, depth // chunks), jnp.bfloat16),
            pltpu.VMEM((n_states, width), jnp.bfloat16),
            pltpu.VMEM((columns, width), jnp.float32),
            pltpu.VMEM((n_row, PIECE, width), jnp.float32),
            pltpu.VMEM((PIECE, width), jnp.bfloat16),
            dma((n_col,)), dma((chunks,)), dma((n_col, chunks)), dma((3, n_col, chunks)),
            dma((pieces,)), dma((n_row,)),
            dma((n_row,)), dma((pieces,)), dma((n_col,)), dma((factor, pieces)),
        ],
        compiler_params=pltpu.CompilerParams(
            collective_id=0, has_side_effects=True, vmem_limit_bytes=48 * 2**20),
        cost_estimate=pl.CostEstimate(
            flops=2 * columns * n_states * width, bytes_accessed=2 * n_states * width, transcendentals=0),
        name="pull",
    )(inverse_slab, pltpu.with_memory_space_constraint(cot_solved, pltpu.HBM))

    panel_width = solved_panel.shape[1]
    tile = min(panel_width, 512)
    tiles = panel_width // tile
    return pl.pallas_call(
        functools.partial(operator_kernel, tile),
        out_shape=(
            jax.ShapeDtypeStruct((columns, width), jnp.float32),
            jax.ShapeDtypeStruct((factor * width, panel_width), jnp.bfloat16),
        ),
        in_specs=[vmem] * 4,
        out_specs=(hbm, hbm),
        scratch_shapes=[
            pltpu.VMEM((factor * width, columns), jnp.bfloat16),
            pltpu.VMEM((columns, width), jnp.float32),
            pltpu.VMEM((tiles, factor * width, tile), jnp.bfloat16),
            dma, dma((tiles,)),
        ],
        compiler_params=pltpu.CompilerParams(vmem_limit_bytes=32 * 2**20),
        cost_estimate=pl.CostEstimate(
            flops=2 * columns * factor * width * panel_width,
            bytes_accessed=2 * factor * width * panel_width, transcendentals=0),
        name="operator",
    )(needed, solved_panel, cot_direct, pulled)


def solution(mesh):
    n_row, n_col = mesh.shape["row"], mesh.shape["col"]
    in_specs = (P("row", "col"), P(None, ("row", "col")), P(None, "col"), P(None, "col"))
    out_specs = (P(None, "col"), P("row", "col"))
    return jax.shard_map(
        functools.partial(body, n_row, n_col),
        mesh=mesh, in_specs=in_specs, out_specs=out_specs, check_vma=False)
```

```python
import functools

import jax
import jax.numpy as jnp
from jax import lax
from jax.experimental import pallas as pl
from jax.experimental.pallas import tpu as pltpu
from jax.sharding import PartitionSpec as P

MESH = pl.DeviceIdType.MESH
PIECE = 16


def when(*conds):
    traced = None
    for cond in conds:
        if cond is not True:
            traced = cond if traced is None else jnp.logical_and(traced, cond)
    if traced is None:
        return lambda body: body()
    return pl.when(traced)


def pull_kernel(n_row, n_col, pieces, chunks,
                inverse_ref, cot_ref, needed_ref, pulled_ref,
                gathered, inverse, part, arrived, low,
                load_sem, own_sem, recv_sem, send_sem, sum_send, sum_recv,
                total_send, total_recv, low_send, low_recv):
    row, col = lax.axis_index("row"), lax.axis_index("col")
    line = n_col // 2
    z, x = col // 2, col % 2
    other = 1 - x
    pair = z * 2 + other
    factor = n_col // n_row
    depth = cot_ref.shape[1]
    span_of = depth // chunks
    balance = line >= 4
    half = chunks // 2
    has_down, has_up = z > 0, z < line - 1

    def load_inverse(block):
        span = pl.ds(pl.multiple_of(block * depth, depth), depth)
        return pltpu.make_async_copy(inverse_ref.at[span], inverse.at[span], load_sem.at[block])

    def load_own(chunk):
        return pltpu.make_async_copy(
            cot_ref.at[:, pl.ds(chunk * span_of, span_of)], gathered.at[col, chunk], own_sem.at[chunk])

    for chunk in range(chunks):
        load_own(chunk).start()

    barrier = pltpu.get_barrier_semaphore()

    def greet(to_row, to_col):
        pl.semaphore_signal(barrier, inc=1, device_id=(to_row, to_col), device_id_type=MESH)

    greet(row, pair)
    pl.when(has_down)(lambda: greet(row, col - 2))
    pl.when(has_up)(lambda: greet(row, col + 2))
    for step in range(1, n_row):
        greet(lax.rem(row + step, n_row), col)

    load_inverse(col).start()
    part[...] = jnp.zeros_like(part)
    for chunk in range(chunks):
        load_own(chunk).wait()
    pl.semaphore_wait(barrier, n_row + has_down.astype(jnp.int32) + has_up.astype(jnp.int32))

    UP, DOWN, ACROSS = 0, 1, 2
    target = {UP: col + 2, DOWN: col - 2, ACROSS: pair}

    def move(stream, block, chunk):
        piece = gathered.at[block, chunk]
        return pltpu.make_async_remote_copy(
            src_ref=piece, dst_ref=piece,
            send_sem=send_sem.at[stream, block, chunk], recv_sem=recv_sem.at[block, chunk],
            device_id=(row, target[stream]), device_id_type=MESH)

    def receive(block, chunk, *conds):
        when(*conds)(lambda: move(ACROSS, block, chunk).wait_recv())

    def multiply(block, which=tuple(range(chunks))):
        if which[0] == 0:
            load_inverse(block).wait()
        total = part[...]
        for chunk in which:
            span = pl.ds(pl.multiple_of(block * depth + chunk * span_of, span_of), span_of)
            total += jnp.dot(
                gathered[block, chunk], inverse[span, :], preferred_element_type=jnp.float32)
        part[...] = total

    sends = []

    def send(stream, block, chunk, *conds):
        when(*conds)(lambda: move(stream, block, chunk).start())
        sends.append((stream, block, chunk, conds))

    def across_ok(of_z, chunk):
        if not balance:
            return ()
        if chunk >= half:
            return of_z != 0, of_z != line - 1
        return (jnp.logical_not(jnp.logical_and(z == 1, of_z == 0)),
                jnp.logical_not(jnp.logical_and(z == line - 2, of_z == line - 1)))

    def take_pair(step):
        for at, there in ((z - 1 - step, z - 1 - step >= 0), (z + 1 + step, z + 1 + step < line)):
            block = at * 2 + other

            @pl.when(there)
            def _():
                for chunk in range(chunks):
                    if balance and chunk >= half:
                        passed_on = jnp.logical_and(
                            jnp.logical_or(at == 0, at == line - 1), jnp.logical_and(has_up, has_down))
                        receive(block, chunk, jnp.logical_not(passed_on))
                    else:
                        receive(block, chunk)
                multiply(block)

    bottom, top = other, (line - 1) * 2 + other

    for chunk in range(chunks):
        send(UP, col, chunk, has_up)
        send(DOWN, col, chunk, has_down)
        send(ACROSS, col, chunk)

    def load_step(step):
        for at, there in ((z - 1 - step, z - 1 - step >= 0), (z + 1 + step, z + 1 + step < line)):
            for side in (x, other):
                pl.when(there)(lambda: load_inverse(at * 2 + side).start())

    load_inverse(pair).start()
    load_step(0)
    multiply(col)

    for step in range(line - 1):
        below, above = z - 1 - step, z + 1 + step
        if step >= 1:
            load_step(step)
        for chunk in range(chunks):
            receive(below * 2 + x, chunk, below >= 0)
            send(UP, below * 2 + x, chunk, below >= 0, has_up)
            send(ACROSS, below * 2 + x, chunk, below >= 0, *across_ok(below, chunk))
            receive(above * 2 + x, chunk, above < line)
            send(DOWN, above * 2 + x, chunk, above < line, has_down)
            send(ACROSS, above * 2 + x, chunk, above < line, *across_ok(above, chunk))
        if balance and step >= 1:
            for chunk in range(half, chunks):
                receive(bottom, chunk, z == step)
                send(UP, bottom, chunk, z == step)
                receive(top, chunk, z == line - 1 - step)
                send(DOWN, top, chunk, z == line - 1 - step)
        pl.when(below >= 0)(lambda: multiply(below * 2 + x))
        pl.when(above < line)(lambda: multiply(above * 2 + x))
        if step == 0:
            for chunk in range(chunks):
                receive(pair, chunk)
                if balance:
                    send(UP, pair, chunk, z == 0)
                    send(DOWN, pair, chunk, z == line - 1)
            multiply(pair)
        else:
            take_pair(step - 1)
    order = [chunk for both in zip(range(half), range(half, chunks)) for chunk in both] if balance else []
    for at, there in ((0, jnp.logical_not(has_up)), (line - 1, jnp.logical_not(has_down))):
        block = at * 2 + other

        @pl.when(there)
        def _():
            for chunk in order or range(chunks):
                receive(block, chunk)
                multiply(block, (chunk,))

    def sum_copy(piece, source):
        return pltpu.make_async_remote_copy(
            src_ref=part.at[pl.ds(piece * PIECE, PIECE), :], dst_ref=arrived.at[source],
            send_sem=sum_send.at[piece], recv_sem=sum_recv.at[source],
            device_id=(piece, col), device_id_type=MESH)

    for piece in range(pieces):
        pl.when(row != piece)(lambda: sum_copy(piece, row).start())

    def total_copy(piece, to_row):
        span = pl.ds(pl.multiple_of(piece * PIECE, PIECE), PIECE)
        return pltpu.make_async_remote_copy(
            src_ref=pulled_ref.at[span, :], dst_ref=pulled_ref.at[span, :],
            send_sem=total_send.at[to_row], recv_sem=total_recv.at[piece],
            device_id=(to_row, col), device_id_type=MESH)

    def low_copy(piece, slot, to_row, to_col):
        span = pl.ds(pl.multiple_of(piece * PIECE, PIECE), PIECE)
        return pltpu.make_async_remote_copy(
            src_ref=low, dst_ref=needed_ref.at[slot, span, :],
            send_sem=low_send.at[to_col], recv_sem=low_recv.at[slot, piece],
            device_id=(to_row, to_col), device_id_type=MESH)

    user, slot = col // factor, col % factor

    @pl.when(row < pieces)
    def _():
        span = pl.ds(pl.multiple_of(row * PIECE, PIECE), PIECE)
        for step in range(1, n_row):
            source = lax.rem(row + step, n_row)
            sum_copy(row, source).wait_recv()
        arrived[row] = part[span, :]
        total = arrived[0]
        for source in range(1, n_row):
            total = total + arrived[source]
        low[...] = total.astype(jnp.bfloat16)
        pulled_ref[span, :] = total
        for to_col in range(n_col):
            mine = jnp.logical_and(user == row, col == to_col)
            pl.when(jnp.logical_not(mine))(lambda: low_copy(row, slot, user, to_col).start())
        for step in range(1, n_row):
            total_copy(row, lax.rem(row + step, n_row)).start()

        @pl.when(user == row)
        def _():
            needed_ref[slot, span, :] = low[...]

    for stream, block, chunk, conds in sends:
        when(*conds)(lambda: move(stream, block, chunk).wait_send())
    for piece in range(pieces):
        pl.when(row != piece)(lambda: sum_copy(piece, row).wait_send())

    @pl.when(row < pieces)
    def _():
        for to_col in range(n_col):
            mine = jnp.logical_and(user == row, col == to_col)
            pl.when(jnp.logical_not(mine))(lambda: low_copy(row, slot, user, to_col).wait_send())
        for step in range(1, n_row):
            total_copy(row, lax.rem(row + step, n_row)).wait_send()

    for piece in range(pieces):
        pl.when(row != piece)(lambda: total_copy(piece, row).wait_recv())
        for at in range(factor):
            mine = jnp.logical_and(row == piece, col == factor * row + at)
            pl.when(jnp.logical_not(mine))(lambda: low_copy(piece, at, row, col).wait_recv())


def operator_kernel(tile, needed_ref, panel_ref, direct_ref, pulled_ref, factor_ref, operator_ref,
                    left, factor, result, factor_sem, result_sem):
    scale = 1.0 / jnp.sqrt(jnp.float32(2.0))
    width = needed_ref.shape[2]
    for at in range(needed_ref.shape[0]):
        left[at * width:(at + 1) * width, :] = needed_ref[at].T

    def store(at):
        span = pl.ds(at * tile, tile)
        return pltpu.make_async_copy(result.at[at], operator_ref.at[:, span], result_sem.at[at])

    tiles = panel_ref.shape[1] // tile
    for at in range(tiles):
        product = jnp.dot(
            left[...], panel_ref[:, at * tile:(at + 1) * tile], preferred_element_type=jnp.float32)
        result[at] = (product * -scale).astype(jnp.bfloat16)
        store(at).start()
        if at == 0:
            factor[...] = (direct_ref[...].astype(jnp.float32) + pulled_ref[...]) * scale
            out = pltpu.make_async_copy(factor, factor_ref, factor_sem)
            out.start()
    for at in range(tiles):
        store(at).wait()
    out.wait()


def body(n_row, n_col, inverse_slab, cot_solved, cot_direct, solved_panel):
    n_states, width = inverse_slab.shape
    columns, depth = cot_solved.shape
    factor = n_col // n_row
    pieces = min(n_row, columns // PIECE)
    chunks = 4 if depth >= 1024 else 1
    hbm = pl.BlockSpec(memory_space=pltpu.HBM)
    vmem = pl.BlockSpec(memory_space=pltpu.VMEM)
    dma = pltpu.SemaphoreType.DMA
    needed, pulled = pl.pallas_call(
        functools.partial(pull_kernel, n_row, n_col, pieces, chunks),
        out_shape=(
            jax.ShapeDtypeStruct((factor, columns, width), jnp.bfloat16),
            jax.ShapeDtypeStruct((columns, width), jnp.float32),
        ),
        in_specs=[hbm, hbm],
        out_specs=(vmem, vmem),
        scratch_shapes=[
            pltpu.VMEM((n_col, chunks, columns, depth // chunks), jnp.bfloat16),
            pltpu.VMEM((n_states, width), jnp.bfloat16),
            pltpu.VMEM((columns, width), jnp.float32),
            pltpu.VMEM((n_row, PIECE, width), jnp.float32),
            pltpu.VMEM((PIECE, width), jnp.bfloat16),
            dma((n_col,)), dma((chunks,)), dma((n_col, chunks)), dma((3, n_col, chunks)),
            dma((pieces,)), dma((n_row,)),
            dma((n_row,)), dma((pieces,)), dma((n_col,)), dma((factor, pieces)),
        ],
        compiler_params=pltpu.CompilerParams(
            collective_id=0, has_side_effects=True, vmem_limit_bytes=48 * 2**20),
        cost_estimate=pl.CostEstimate(
            flops=2 * columns * n_states * width, bytes_accessed=2 * n_states * width, transcendentals=0),
        name="pull",
    )(inverse_slab, pltpu.with_memory_space_constraint(cot_solved, pltpu.HBM))

    panel_width = solved_panel.shape[1]
    tile = min(panel_width, 512)
    tiles = panel_width // tile
    return pl.pallas_call(
        functools.partial(operator_kernel, tile),
        out_shape=(
            jax.ShapeDtypeStruct((columns, width), jnp.float32),
            jax.ShapeDtypeStruct((factor * width, panel_width), jnp.bfloat16),
        ),
        in_specs=[vmem] * 4,
        out_specs=(hbm, hbm),
        scratch_shapes=[
            pltpu.VMEM((factor * width, columns), jnp.bfloat16),
            pltpu.VMEM((columns, width), jnp.float32),
            pltpu.VMEM((tiles, factor * width, tile), jnp.bfloat16),
            dma, dma((tiles,)),
        ],
        compiler_params=pltpu.CompilerParams(vmem_limit_bytes=32 * 2**20),
        cost_estimate=pl.CostEstimate(
            flops=2 * columns * factor * width * panel_width,
            bytes_accessed=2 * factor * width * panel_width, transcendentals=0),
        name="operator",
    )(needed, solved_panel, cot_direct, pulled)


def solution(mesh):
    n_row, n_col = mesh.shape["row"], mesh.shape["col"]
    in_specs = (P("row", "col"), P(None, ("row", "col")), P(None, "col"), P(None, "col"))
    out_specs = (P(None, "col"), P("row", "col"))
    return jax.shard_map(
        functools.partial(body, n_row, n_col),
        mesh=mesh, in_specs=in_specs, out_specs=out_specs, check_vma=False)
```

```python
import functools

import jax
import jax.numpy as jnp
from jax import lax
from jax.experimental import pallas as pl
from jax.experimental.pallas import tpu as pltpu
from jax.sharding import PartitionSpec as P

MESH = pl.DeviceIdType.MESH
PIECE = 16


def when(*conds):
    traced = None
    for cond in conds:
        if cond is not True:
            traced = cond if traced is None else jnp.logical_and(traced, cond)
    if traced is None:
        return lambda body: body()
    return pl.when(traced)


def pull_kernel(n_row, n_col, pieces, chunks,
                inverse_ref, cot_ref, needed_ref, pulled_ref,
                gathered, inverse, part, arrived, low,
                load_sem, own_sem, recv_sem, send_sem, sum_send, sum_recv,
                total_send, total_recv, low_send, low_recv):
    row, col = lax.axis_index("row"), lax.axis_index("col")
    line = n_col // 2
    z, x = col // 2, col % 2
    other = 1 - x
    pair = z * 2 + other
    factor = n_col // n_row
    depth = cot_ref.shape[1]
    span_of = depth // chunks
    balance = line >= 4
    half = chunks // 2
    has_down, has_up = z > 0, z < line - 1

    def load_inverse(block):
        span = pl.ds(pl.multiple_of(block * depth, depth), depth)
        return pltpu.make_async_copy(inverse_ref.at[span], inverse.at[span], load_sem.at[block])

    def load_own(chunk):
        return pltpu.make_async_copy(
            cot_ref.at[:, pl.ds(chunk * span_of, span_of)], gathered.at[col, chunk], own_sem.at[chunk])

    for chunk in range(chunks):
        load_own(chunk).start()

    barrier = pltpu.get_barrier_semaphore()

    def greet(to_row, to_col):
        pl.semaphore_signal(barrier, inc=1, device_id=(to_row, to_col), device_id_type=MESH)

    greet(row, pair)
    pl.when(has_down)(lambda: greet(row, col - 2))
    pl.when(has_up)(lambda: greet(row, col + 2))
    for step in range(1, n_row):
        greet(lax.rem(row + step, n_row), col)

    load_inverse(col).start()
    part[...] = jnp.zeros_like(part)
    for chunk in range(chunks):
        load_own(chunk).wait()
    pl.semaphore_wait(barrier, n_row + has_down.astype(jnp.int32) + has_up.astype(jnp.int32))

    UP, DOWN, ACROSS = 0, 1, 2
    target = {UP: col + 2, DOWN: col - 2, ACROSS: pair}

    def move(stream, block, chunk):
        piece = gathered.at[block, chunk]
        return pltpu.make_async_remote_copy(
            src_ref=piece, dst_ref=piece,
            send_sem=send_sem.at[stream, block, chunk], recv_sem=recv_sem.at[block, chunk],
            device_id=(row, target[stream]), device_id_type=MESH)

    def receive(block, chunk, *conds):
        when(*conds)(lambda: move(ACROSS, block, chunk).wait_recv())

    def multiply(block, which=tuple(range(chunks))):
        if which[0] == 0:
            load_inverse(block).wait()
        total = part[...]
        for chunk in which:
            span = pl.ds(pl.multiple_of(block * depth + chunk * span_of, span_of), span_of)
            total += jnp.dot(
                gathered[block, chunk], inverse[span, :], preferred_element_type=jnp.float32)
        part[...] = total

    sends = []

    def send(stream, block, chunk, *conds):
        when(*conds)(lambda: move(stream, block, chunk).start())
        sends.append((stream, block, chunk, conds))

    def across_ok(of_z, chunk):
        if not balance:
            return ()
        if chunk >= half:
            return of_z != 0, of_z != line - 1
        return (jnp.logical_not(jnp.logical_and(z == 1, of_z == 0)),
                jnp.logical_not(jnp.logical_and(z == line - 2, of_z == line - 1)))

    def take_pair(step):
        for at, there in ((z - 1 - step, z - 1 - step >= 0), (z + 1 + step, z + 1 + step < line)):
            block = at * 2 + other

            @pl.when(there)
            def _():
                for chunk in range(chunks):
                    if balance and chunk >= half:
                        passed_on = jnp.logical_and(
                            jnp.logical_or(at == 0, at == line - 1), jnp.logical_and(has_up, has_down))
                        receive(block, chunk, jnp.logical_not(passed_on))
                    else:
                        receive(block, chunk)
                multiply(block)

    bottom, top = other, (line - 1) * 2 + other

    for chunk in range(chunks):
        send(UP, col, chunk, has_up)
        send(DOWN, col, chunk, has_down)
        send(ACROSS, col, chunk)

    def load_step(step):
        for at, there in ((z - 1 - step, z - 1 - step >= 0), (z + 1 + step, z + 1 + step < line)):
            for side in (x, other):
                pl.when(there)(lambda: load_inverse(at * 2 + side).start())

    load_inverse(pair).start()
    load_step(0)
    multiply(col)

    for step in range(line - 1):
        below, above = z - 1 - step, z + 1 + step
        if step >= 1:
            load_step(step)
        for chunk in range(chunks):
            receive(below * 2 + x, chunk, below >= 0)
            send(UP, below * 2 + x, chunk, below >= 0, has_up)
            send(ACROSS, below * 2 + x, chunk, below >= 0, *across_ok(below, chunk))
            receive(above * 2 + x, chunk, above < line)
            send(DOWN, above * 2 + x, chunk, above < line, has_down)
            send(ACROSS, above * 2 + x, chunk, above < line, *across_ok(above, chunk))
        if balance and step >= 1:
            for chunk in range(half, chunks):
                receive(bottom, chunk, z == step)
                send(UP, bottom, chunk, z == step)
                receive(top, chunk, z == line - 1 - step)
                send(DOWN, top, chunk, z == line - 1 - step)
        pl.when(below >= 0)(lambda: multiply(below * 2 + x))
        pl.when(above < line)(lambda: multiply(above * 2 + x))
        if step == 0:
            for chunk in range(chunks):
                receive(pair, chunk)
                if balance:
                    send(UP, pair, chunk, z == 0)
                    send(DOWN, pair, chunk, z == line - 1)
            multiply(pair)
        else:
            take_pair(step - 1)
    order = [chunk for both in zip(range(half), range(half, chunks)) for chunk in both] if balance else []
    for at, there in ((0, jnp.logical_not(has_up)), (line - 1, jnp.logical_not(has_down))):
        block = at * 2 + other

        @pl.when(there)
        def _():
            for chunk in order or range(chunks):
                receive(block, chunk)
                multiply(block, (chunk,))

    def sum_copy(piece, source):
        return pltpu.make_async_remote_copy(
            src_ref=part.at[pl.ds(piece * PIECE, PIECE), :], dst_ref=arrived.at[source],
            send_sem=sum_send.at[piece], recv_sem=sum_recv.at[source],
            device_id=(piece, col), device_id_type=MESH)

    for piece in range(pieces):
        pl.when(row != piece)(lambda: sum_copy(piece, row).start())

    def total_copy(piece, to_row):
        span = pl.ds(pl.multiple_of(piece * PIECE, PIECE), PIECE)
        return pltpu.make_async_remote_copy(
            src_ref=pulled_ref.at[span, :], dst_ref=pulled_ref.at[span, :],
            send_sem=total_send.at[to_row], recv_sem=total_recv.at[piece],
            device_id=(to_row, col), device_id_type=MESH)

    def low_copy(piece, slot, to_row, to_col):
        span = pl.ds(pl.multiple_of(piece * PIECE, PIECE), PIECE)
        return pltpu.make_async_remote_copy(
            src_ref=low, dst_ref=needed_ref.at[slot, span, :],
            send_sem=low_send.at[to_col], recv_sem=low_recv.at[slot, piece],
            device_id=(to_row, to_col), device_id_type=MESH)

    user, slot = col // factor, col % factor

    @pl.when(row < pieces)
    def _():
        span = pl.ds(pl.multiple_of(row * PIECE, PIECE), PIECE)
        for step in range(1, n_row):
            source = lax.rem(row + step, n_row)
            sum_copy(row, source).wait_recv()
        arrived[row] = part[span, :]
        total = arrived[0]
        for source in range(1, n_row):
            total = total + arrived[source]
        low[...] = total.astype(jnp.bfloat16)
        pulled_ref[span, :] = total
        for to_col in range(n_col):
            mine = jnp.logical_and(user == row, col == to_col)
            pl.when(jnp.logical_not(mine))(lambda: low_copy(row, slot, user, to_col).start())
        for step in range(1, n_row):
            total_copy(row, lax.rem(row + step, n_row)).start()

        @pl.when(user == row)
        def _():
            needed_ref[slot, span, :] = low[...]

    for stream, block, chunk, conds in sends:
        when(*conds)(lambda: move(stream, block, chunk).wait_send())
    for piece in range(pieces):
        pl.when(row != piece)(lambda: sum_copy(piece, row).wait_send())

    @pl.when(row < pieces)
    def _():
        for to_col in range(n_col):
            mine = jnp.logical_and(user == row, col == to_col)
            pl.when(jnp.logical_not(mine))(lambda: low_copy(row, slot, user, to_col).wait_send())
        for step in range(1, n_row):
            total_copy(row, lax.rem(row + step, n_row)).wait_send()

    for piece in range(pieces):
        pl.when(row != piece)(lambda: total_copy(piece, row).wait_recv())
        for at in range(factor):
            mine = jnp.logical_and(row == piece, col == factor * row + at)
            pl.when(jnp.logical_not(mine))(lambda: low_copy(piece, at, row, col).wait_recv())


def operator_kernel(tile, needed_ref, panel_ref, direct_ref, pulled_ref, factor_ref, operator_ref,
                    left, factor, result, factor_sem, result_sem):
    scale = 1.0 / jnp.sqrt(jnp.float32(2.0))
    width = needed_ref.shape[2]
    for at in range(needed_ref.shape[0]):
        left[at * width:(at + 1) * width, :] = needed_ref[at].T

    def store(at):
        span = pl.ds(at * tile, tile)
        return pltpu.make_async_copy(result.at[at], operator_ref.at[:, span], result_sem.at[at])

    tiles = panel_ref.shape[1] // tile
    for at in range(tiles):
        product = jnp.dot(
            left[...], panel_ref[:, at * tile:(at + 1) * tile], preferred_element_type=jnp.float32)
        result[at] = (product * -scale).astype(jnp.bfloat16)
        store(at).start()
        if at == 0:
            factor[...] = (direct_ref[...].astype(jnp.float32) + pulled_ref[...]) * scale
            out = pltpu.make_async_copy(factor, factor_ref, factor_sem)
            out.start()
    for at in range(tiles):
        store(at).wait()
    out.wait()


def body(n_row, n_col, inverse_slab, cot_solved, cot_direct, solved_panel):
    n_states, width = inverse_slab.shape
    columns, depth = cot_solved.shape
    factor = n_col // n_row
    pieces = min(n_row, columns // PIECE)
    chunks = 2 if depth >= 1024 else 1
    hbm = pl.BlockSpec(memory_space=pltpu.HBM)
    vmem = pl.BlockSpec(memory_space=pltpu.VMEM)
    dma = pltpu.SemaphoreType.DMA
    needed, pulled = pl.pallas_call(
        functools.partial(pull_kernel, n_row, n_col, pieces, chunks),
        out_shape=(
            jax.ShapeDtypeStruct((factor, columns, width), jnp.bfloat16),
            jax.ShapeDtypeStruct((columns, width), jnp.float32),
        ),
        in_specs=[hbm, hbm],
        out_specs=(vmem, vmem),
        scratch_shapes=[
            pltpu.VMEM((n_col, chunks, columns, depth // chunks), jnp.bfloat16),
            pltpu.VMEM((n_states, width), jnp.bfloat16),
            pltpu.VMEM((columns, width), jnp.float32),
            pltpu.VMEM((n_row, PIECE, width), jnp.float32),
            pltpu.VMEM((PIECE, width), jnp.bfloat16),
            dma((n_col,)), dma((chunks,)), dma((n_col, chunks)), dma((3, n_col, chunks)),
            dma((pieces,)), dma((n_row,)),
            dma((n_row,)), dma((pieces,)), dma((n_col,)), dma((factor, pieces)),
        ],
        compiler_params=pltpu.CompilerParams(
            collective_id=0, has_side_effects=True, vmem_limit_bytes=48 * 2**20),
        cost_estimate=pl.CostEstimate(
            flops=2 * columns * n_states * width, bytes_accessed=2 * n_states * width, transcendentals=0),
        name="pull",
    )(inverse_slab, pltpu.with_memory_space_constraint(cot_solved, pltpu.HBM))

    panel_width = solved_panel.shape[1]
    tile = min(panel_width, 1024)
    tiles = panel_width // tile
    return pl.pallas_call(
        functools.partial(operator_kernel, tile),
        out_shape=(
            jax.ShapeDtypeStruct((columns, width), jnp.float32),
            jax.ShapeDtypeStruct((factor * width, panel_width), jnp.bfloat16),
        ),
        in_specs=[vmem] * 4,
        out_specs=(hbm, hbm),
        scratch_shapes=[
            pltpu.VMEM((factor * width, columns), jnp.bfloat16),
            pltpu.VMEM((columns, width), jnp.float32),
            pltpu.VMEM((tiles, factor * width, tile), jnp.bfloat16),
            dma, dma((tiles,)),
        ],
        compiler_params=pltpu.CompilerParams(vmem_limit_bytes=32 * 2**20),
        cost_estimate=pl.CostEstimate(
            flops=2 * columns * factor * width * panel_width,
            bytes_accessed=2 * factor * width * panel_width, transcendentals=0),
        name="operator",
    )(needed, solved_panel, cot_direct, pulled)


def solution(mesh):
    n_row, n_col = mesh.shape["row"], mesh.shape["col"]
    in_specs = (P("row", "col"), P(None, ("row", "col")), P(None, "col"), P(None, "col"))
    out_specs = (P(None, "col"), P("row", "col"))
    return jax.shard_map(
        functools.partial(body, n_row, n_col),
        mesh=mesh, in_specs=in_specs, out_specs=out_specs, check_vma=False)
```

```python
import functools

import jax
import jax.numpy as jnp
from jax import lax
from jax.experimental import pallas as pl
from jax.experimental.pallas import tpu as pltpu
from jax.sharding import PartitionSpec as P

MESH = pl.DeviceIdType.MESH
PIECE = 16


def when(*conds):
    traced = None
    for cond in conds:
        if cond is not True:
            traced = cond if traced is None else jnp.logical_and(traced, cond)
    if traced is None:
        return lambda body: body()
    return pl.when(traced)


def pull_kernel(n_row, n_col, pieces, chunks,
                inverse_ref, cot_ref, needed_ref, pulled_ref,
                gathered, inverse, part, arrived, low,
                load_sem, own_sem, recv_sem, send_sem, sum_send, sum_recv,
                total_send, total_recv, low_send, low_recv):
    row, col = lax.axis_index("row"), lax.axis_index("col")
    line = n_col // 2
    z, x = col // 2, col % 2
    other = 1 - x
    pair = z * 2 + other
    factor = n_col // n_row
    depth = cot_ref.shape[1]
    span_of = depth // chunks
    balance = line >= 4
    half = chunks // 2
    has_down, has_up = z > 0, z < line - 1

    def load_inverse(block):
        span = pl.ds(pl.multiple_of(block * depth, depth), depth)
        return pltpu.make_async_copy(inverse_ref.at[span], inverse.at[span], load_sem.at[block])

    def load_own(chunk):
        return pltpu.make_async_copy(
            cot_ref.at[:, pl.ds(chunk * span_of, span_of)], gathered.at[col, chunk], own_sem.at[chunk])

    for chunk in range(chunks):
        load_own(chunk).start()

    barrier = pltpu.get_barrier_semaphore()

    def greet(to_row, to_col):
        pl.semaphore_signal(barrier, inc=1, device_id=(to_row, to_col), device_id_type=MESH)

    greet(row, pair)
    pl.when(has_down)(lambda: greet(row, col - 2))
    pl.when(has_up)(lambda: greet(row, col + 2))
    for step in range(1, n_row):
        greet(lax.rem(row + step, n_row), col)

    load_inverse(col).start()
    part[...] = jnp.zeros_like(part)
    for chunk in range(chunks):
        load_own(chunk).wait()
    pl.semaphore_wait(barrier, n_row + has_down.astype(jnp.int32) + has_up.astype(jnp.int32))

    UP, DOWN, ACROSS = 0, 1, 2
    target = {UP: col + 2, DOWN: col - 2, ACROSS: pair}

    def move(stream, block, chunk):
        piece = gathered.at[block, chunk]
        return pltpu.make_async_remote_copy(
            src_ref=piece, dst_ref=piece,
            send_sem=send_sem.at[stream, block, chunk], recv_sem=recv_sem.at[block, chunk],
            device_id=(row, target[stream]), device_id_type=MESH)

    def receive(block, chunk, *conds):
        when(*conds)(lambda: move(ACROSS, block, chunk).wait_recv())

    def multiply(block, which=tuple(range(chunks))):
        if which[0] == 0:
            load_inverse(block).wait()
        total = part[...]
        for chunk in which:
            span = pl.ds(pl.multiple_of(block * depth + chunk * span_of, span_of), span_of)
            total += jnp.dot(
                gathered[block, chunk], inverse[span, :], preferred_element_type=jnp.float32)
        part[...] = total

    sends = []

    def send(stream, block, chunk, *conds):
        when(*conds)(lambda: move(stream, block, chunk).start())
        sends.append((stream, block, chunk, conds))

    def across_ok(of_z, chunk):
        if not balance:
            return ()
        if chunk >= half:
            return of_z != 0, of_z != line - 1
        return (jnp.logical_not(jnp.logical_and(z == 1, of_z == 0)),
                jnp.logical_not(jnp.logical_and(z == line - 2, of_z == line - 1)))

    def take_pair(step):
        for at, there in ((z - 1 - step, z - 1 - step >= 0), (z + 1 + step, z + 1 + step < line)):
            block = at * 2 + other

            @pl.when(there)
            def _():
                for chunk in range(chunks):
                    if balance and chunk >= half:
                        passed_on = jnp.logical_and(
                            jnp.logical_or(at == 0, at == line - 1), jnp.logical_and(has_up, has_down))
                        receive(block, chunk, jnp.logical_not(passed_on))
                    else:
                        receive(block, chunk)
                multiply(block)

    bottom, top = other, (line - 1) * 2 + other

    def send_own(chunk):
        send(UP, col, chunk, has_up)
        send(DOWN, col, chunk, has_down)
        send(ACROSS, col, chunk)

    window = max(half, 1)
    for chunk in range(window):
        send_own(chunk)

    def load_step(step):
        for at, there in ((z - 1 - step, z - 1 - step >= 0), (z + 1 + step, z + 1 + step < line)):
            for side in (x, other):
                pl.when(there)(lambda: load_inverse(at * 2 + side).start())

    load_inverse(pair).start()
    load_step(0)
    multiply(col)
    for chunk in range(window, chunks):
        for stream, conds in ((UP, (has_up,)), (DOWN, (has_down,))):
            when(*conds)(lambda: move(stream, col, chunk - window).wait_send())
            sends.remove((stream, col, chunk - window, conds))
        send_own(chunk)

    for step in range(line - 1):
        below, above = z - 1 - step, z + 1 + step
        if step >= 1:
            load_step(step)
        for chunk in range(chunks):
            receive(below * 2 + x, chunk, below >= 0)
            send(UP, below * 2 + x, chunk, below >= 0, has_up)
            send(ACROSS, below * 2 + x, chunk, below >= 0, *across_ok(below, chunk))
            receive(above * 2 + x, chunk, above < line)
            send(DOWN, above * 2 + x, chunk, above < line, has_down)
            send(ACROSS, above * 2 + x, chunk, above < line, *across_ok(above, chunk))
        if balance and step >= 1:
            for chunk in range(half, chunks):
                receive(bottom, chunk, z == step)
                send(UP, bottom, chunk, z == step)
                receive(top, chunk, z == line - 1 - step)
                send(DOWN, top, chunk, z == line - 1 - step)
        pl.when(below >= 0)(lambda: multiply(below * 2 + x))
        pl.when(above < line)(lambda: multiply(above * 2 + x))
        if step == 0:
            for chunk in range(chunks):
                receive(pair, chunk)
                if balance:
                    send(UP, pair, chunk, z == 0)
                    send(DOWN, pair, chunk, z == line - 1)
            multiply(pair)
        else:
            take_pair(step - 1)
    order = [chunk for both in zip(range(half), range(half, chunks)) for chunk in both] if balance else []
    for at, there in ((0, jnp.logical_not(has_up)), (line - 1, jnp.logical_not(has_down))):
        block = at * 2 + other

        @pl.when(there)
        def _():
            for chunk in order or range(chunks):
                receive(block, chunk)
                multiply(block, (chunk,))

    def sum_copy(piece, source):
        return pltpu.make_async_remote_copy(
            src_ref=part.at[pl.ds(piece * PIECE, PIECE), :], dst_ref=arrived.at[source],
            send_sem=sum_send.at[piece], recv_sem=sum_recv.at[source],
            device_id=(piece, col), device_id_type=MESH)

    for piece in range(pieces):
        pl.when(row != piece)(lambda: sum_copy(piece, row).start())

    def total_copy(piece, to_row):
        span = pl.ds(pl.multiple_of(piece * PIECE, PIECE), PIECE)
        return pltpu.make_async_remote_copy(
            src_ref=pulled_ref.at[span, :], dst_ref=pulled_ref.at[span, :],
            send_sem=total_send.at[to_row], recv_sem=total_recv.at[piece],
            device_id=(to_row, col), device_id_type=MESH)

    def low_copy(piece, slot, to_row, to_col):
        span = pl.ds(pl.multiple_of(piece * PIECE, PIECE), PIECE)
        return pltpu.make_async_remote_copy(
            src_ref=low, dst_ref=needed_ref.at[slot, span, :],
            send_sem=low_send.at[to_col], recv_sem=low_recv.at[slot, piece],
            device_id=(to_row, to_col), device_id_type=MESH)

    user, slot = col // factor, col % factor

    @pl.when(row < pieces)
    def _():
        span = pl.ds(pl.multiple_of(row * PIECE, PIECE), PIECE)
        for step in range(1, n_row):
            source = lax.rem(row + step, n_row)
            sum_copy(row, source).wait_recv()
        arrived[row] = part[span, :]
        total = arrived[0]
        for source in range(1, n_row):
            total = total + arrived[source]
        low[...] = total.astype(jnp.bfloat16)
        pulled_ref[span, :] = total
        for to_col in range(n_col):
            mine = jnp.logical_and(user == row, col == to_col)
            pl.when(jnp.logical_not(mine))(lambda: low_copy(row, slot, user, to_col).start())
        for step in range(1, n_row):
            total_copy(row, lax.rem(row + step, n_row)).start()

        @pl.when(user == row)
        def _():
            needed_ref[slot, span, :] = low[...]

    for stream, block, chunk, conds in sends:
        when(*conds)(lambda: move(stream, block, chunk).wait_send())
    for piece in range(pieces):
        pl.when(row != piece)(lambda: sum_copy(piece, row).wait_send())

    @pl.when(row < pieces)
    def _():
        for to_col in range(n_col):
            mine = jnp.logical_and(user == row, col == to_col)
            pl.when(jnp.logical_not(mine))(lambda: low_copy(row, slot, user, to_col).wait_send())
        for step in range(1, n_row):
            total_copy(row, lax.rem(row + step, n_row)).wait_send()

    for piece in range(pieces):
        pl.when(row != piece)(lambda: total_copy(piece, row).wait_recv())
        for at in range(factor):
            mine = jnp.logical_and(row == piece, col == factor * row + at)
            pl.when(jnp.logical_not(mine))(lambda: low_copy(piece, at, row, col).wait_recv())


def operator_kernel(tile, needed_ref, panel_ref, direct_ref, pulled_ref, factor_ref, operator_ref,
                    left, factor, result, factor_sem, result_sem):
    scale = 1.0 / jnp.sqrt(jnp.float32(2.0))
    width = needed_ref.shape[2]
    for at in range(needed_ref.shape[0]):
        left[at * width:(at + 1) * width, :] = needed_ref[at].T

    def store(at):
        span = pl.ds(at * tile, tile)
        return pltpu.make_async_copy(result.at[at], operator_ref.at[:, span], result_sem.at[at])

    tiles = panel_ref.shape[1] // tile
    for at in range(tiles):
        product = jnp.dot(
            left[...], panel_ref[:, at * tile:(at + 1) * tile], preferred_element_type=jnp.float32)
        result[at] = (product * -scale).astype(jnp.bfloat16)
        store(at).start()
        if at == 0:
            factor[...] = (direct_ref[...].astype(jnp.float32) + pulled_ref[...]) * scale
            out = pltpu.make_async_copy(factor, factor_ref, factor_sem)
            out.start()
    for at in range(tiles):
        store(at).wait()
    out.wait()


def body(n_row, n_col, inverse_slab, cot_solved, cot_direct, solved_panel):
    n_states, width = inverse_slab.shape
    columns, depth = cot_solved.shape
    factor = n_col // n_row
    pieces = min(n_row, columns // PIECE)
    chunks = 4 if depth >= 1024 else 1
    hbm = pl.BlockSpec(memory_space=pltpu.HBM)
    vmem = pl.BlockSpec(memory_space=pltpu.VMEM)
    dma = pltpu.SemaphoreType.DMA
    needed, pulled = pl.pallas_call(
        functools.partial(pull_kernel, n_row, n_col, pieces, chunks),
        out_shape=(
            jax.ShapeDtypeStruct((factor, columns, width), jnp.bfloat16),
            jax.ShapeDtypeStruct((columns, width), jnp.float32),
        ),
        in_specs=[hbm, hbm],
        out_specs=(vmem, vmem),
        scratch_shapes=[
            pltpu.VMEM((n_col, chunks, columns, depth // chunks), jnp.bfloat16),
            pltpu.VMEM((n_states, width), jnp.bfloat16),
            pltpu.VMEM((columns, width), jnp.float32),
            pltpu.VMEM((n_row, PIECE, width), jnp.float32),
            pltpu.VMEM((PIECE, width), jnp.bfloat16),
            dma((n_col,)), dma((chunks,)), dma((n_col, chunks)), dma((3, n_col, chunks)),
            dma((pieces,)), dma((n_row,)),
            dma((n_row,)), dma((pieces,)), dma((n_col,)), dma((factor, pieces)),
        ],
        compiler_params=pltpu.CompilerParams(
            collective_id=0, has_side_effects=True, vmem_limit_bytes=48 * 2**20),
        cost_estimate=pl.CostEstimate(
            flops=2 * columns * n_states * width, bytes_accessed=2 * n_states * width, transcendentals=0),
        name="pull",
    )(inverse_slab, pltpu.with_memory_space_constraint(cot_solved, pltpu.HBM))

    panel_width = solved_panel.shape[1]
    tile = min(panel_width, 256)
    tiles = panel_width // tile
    return pl.pallas_call(
        functools.partial(operator_kernel, tile),
        out_shape=(
            jax.ShapeDtypeStruct((columns, width), jnp.float32),
            jax.ShapeDtypeStruct((factor * width, panel_width), jnp.bfloat16),
        ),
        in_specs=[vmem] * 4,
        out_specs=(hbm, hbm),
        scratch_shapes=[
            pltpu.VMEM((factor * width, columns), jnp.bfloat16),
            pltpu.VMEM((columns, width), jnp.float32),
            pltpu.VMEM((tiles, factor * width, tile), jnp.bfloat16),
            dma, dma((tiles,)),
        ],
        compiler_params=pltpu.CompilerParams(vmem_limit_bytes=32 * 2**20),
        cost_estimate=pl.CostEstimate(
            flops=2 * columns * factor * width * panel_width,
            bytes_accessed=2 * factor * width * panel_width, transcendentals=0),
        name="operator",
    )(needed, solved_panel, cot_direct, pulled)


def solution(mesh):
    n_row, n_col = mesh.shape["row"], mesh.shape["col"]
    in_specs = (P("row", "col"), P(None, ("row", "col")), P(None, "col"), P(None, "col"))
    out_specs = (P(None, "col"), P("row", "col"))
    return jax.shard_map(
        functools.partial(body, n_row, n_col),
        mesh=mesh, in_specs=in_specs, out_specs=out_specs, check_vma=False)
```

```python
import functools

import jax
import jax.numpy as jnp
from jax import lax
from jax.experimental import pallas as pl
from jax.experimental.pallas import tpu as pltpu
from jax.sharding import PartitionSpec as P

MESH = pl.DeviceIdType.MESH
PIECE = 16


def when(*conds):
    traced = None
    for cond in conds:
        if cond is not True:
            traced = cond if traced is None else jnp.logical_and(traced, cond)
    if traced is None:
        return lambda body: body()
    return pl.when(traced)


def pull_kernel(n_row, n_col, pieces, chunks,
                inverse_ref, cot_ref, needed_ref, pulled_ref,
                gathered, inverse, part, arrived, low,
                load_sem, own_sem, recv_sem, send_sem, sum_send, sum_recv,
                total_send, total_recv, low_send, low_recv):
    row, col = lax.axis_index("row"), lax.axis_index("col")
    line = n_col // 2
    z, x = col // 2, col % 2
    other = 1 - x
    pair = z * 2 + other
    factor = n_col // n_row
    depth = cot_ref.shape[1]
    span_of = depth // chunks
    balance = line >= 4
    split = chunks
    has_down, has_up = z > 0, z < line - 1

    def load_inverse(block):
        span = pl.ds(pl.multiple_of(block * depth, depth), depth)
        return pltpu.make_async_copy(inverse_ref.at[span], inverse.at[span], load_sem.at[block])

    def load_own(chunk):
        return pltpu.make_async_copy(
            cot_ref.at[:, pl.ds(chunk * span_of, span_of)], gathered.at[col, chunk], own_sem.at[chunk])

    for chunk in range(chunks):
        load_own(chunk).start()

    barrier = pltpu.get_barrier_semaphore()

    def greet(to_row, to_col):
        pl.semaphore_signal(barrier, inc=1, device_id=(to_row, to_col), device_id_type=MESH)

    greet(row, pair)
    pl.when(has_down)(lambda: greet(row, col - 2))
    pl.when(has_up)(lambda: greet(row, col + 2))
    for step in range(1, n_row):
        greet(lax.rem(row + step, n_row), col)

    load_inverse(col).start()
    part[...] = jnp.zeros_like(part)
    for chunk in range(chunks):
        load_own(chunk).wait()
    pl.semaphore_wait(barrier, n_row + has_down.astype(jnp.int32) + has_up.astype(jnp.int32))

    UP, DOWN, ACROSS = 0, 1, 2
    target = {UP: col + 2, DOWN: col - 2, ACROSS: pair}

    def move(stream, block, chunk):
        piece = gathered.at[block, chunk]
        return pltpu.make_async_remote_copy(
            src_ref=piece, dst_ref=piece,
            send_sem=send_sem.at[stream, block, chunk], recv_sem=recv_sem.at[block, chunk],
            device_id=(row, target[stream]), device_id_type=MESH)

    def receive(block, chunk, *conds):
        when(*conds)(lambda: move(ACROSS, block, chunk).wait_recv())

    def multiply(block, which=tuple(range(chunks))):
        if which[0] == 0:
            load_inverse(block).wait()
        total = part[...]
        for chunk in which:
            span = pl.ds(pl.multiple_of(block * depth + chunk * span_of, span_of), span_of)
            total += jnp.dot(
                gathered[block, chunk], inverse[span, :], preferred_element_type=jnp.float32)
        part[...] = total

    sends = []

    def send(stream, block, chunk, *conds):
        when(*conds)(lambda: move(stream, block, chunk).start())
        sends.append((stream, block, chunk, conds))

    def across_ok(of_z, chunk):
        if not balance:
            return ()
        if chunk >= split:
            return of_z != 0, of_z != line - 1
        return (jnp.logical_not(jnp.logical_and(z == 1, of_z == 0)),
                jnp.logical_not(jnp.logical_and(z == line - 2, of_z == line - 1)))

    def take_pair(step):
        for at, there in ((z - 1 - step, z - 1 - step >= 0), (z + 1 + step, z + 1 + step < line)):
            block = at * 2 + other

            @pl.when(there)
            def _():
                for chunk in range(chunks):
                    if balance and chunk >= split:
                        passed_on = jnp.logical_and(
                            jnp.logical_or(at == 0, at == line - 1), jnp.logical_and(has_up, has_down))
                        receive(block, chunk, jnp.logical_not(passed_on))
                    else:
                        receive(block, chunk)
                multiply(block)

    bottom, top = other, (line - 1) * 2 + other

    def send_own(chunk):
        send(UP, col, chunk, has_up)
        send(DOWN, col, chunk, has_down)
        send(ACROSS, col, chunk)

    for chunk in range(chunks):
        send_own(chunk)

    def load_step(step):
        for at, there in ((z - 1 - step, z - 1 - step >= 0), (z + 1 + step, z + 1 + step < line)):
            for side in (x, other):
                pl.when(there)(lambda: load_inverse(at * 2 + side).start())

    load_inverse(pair).start()
    load_step(0)
    multiply(col)

    for step in range(line - 1):
        below, above = z - 1 - step, z + 1 + step
        if step >= 1:
            load_step(step)
        for chunk in range(chunks):
            receive(below * 2 + x, chunk, below >= 0)
            send(UP, below * 2 + x, chunk, below >= 0, has_up)
            send(ACROSS, below * 2 + x, chunk, below >= 0, *across_ok(below, chunk))
            receive(above * 2 + x, chunk, above < line)
            send(DOWN, above * 2 + x, chunk, above < line, has_down)
            send(ACROSS, above * 2 + x, chunk, above < line, *across_ok(above, chunk))
        if balance and step >= 1:
            for chunk in range(split, chunks):
                receive(bottom, chunk, z == step)
                send(UP, bottom, chunk, z == step)
                receive(top, chunk, z == line - 1 - step)
                send(DOWN, top, chunk, z == line - 1 - step)
        pl.when(below >= 0)(lambda: multiply(below * 2 + x))
        pl.when(above < line)(lambda: multiply(above * 2 + x))
        if step == 0:
            for chunk in range(chunks):
                receive(pair, chunk)
                if balance:
                    send(UP, pair, chunk, z == 0)
                    send(DOWN, pair, chunk, z == line - 1)
            multiply(pair)
        else:
            take_pair(step - 1)
    for at, there in ((0, jnp.logical_not(has_up)), (line - 1, jnp.logical_not(has_down))):
        block = at * 2 + other

        @pl.when(there)
        def _():
            for chunk in range(chunks):
                receive(block, chunk)
                multiply(block, (chunk,))

    def sum_copy(piece, source):
        return pltpu.make_async_remote_copy(
            src_ref=part.at[pl.ds(piece * PIECE, PIECE), :], dst_ref=arrived.at[source],
            send_sem=sum_send.at[piece], recv_sem=sum_recv.at[source],
            device_id=(piece, col), device_id_type=MESH)

    for piece in range(pieces):
        pl.when(row != piece)(lambda: sum_copy(piece, row).start())

    def total_copy(piece, to_row):
        span = pl.ds(pl.multiple_of(piece * PIECE, PIECE), PIECE)
        return pltpu.make_async_remote_copy(
            src_ref=pulled_ref.at[span, :], dst_ref=pulled_ref.at[span, :],
            send_sem=total_send.at[to_row], recv_sem=total_recv.at[piece],
            device_id=(to_row, col), device_id_type=MESH)

    def low_copy(piece, slot, to_row, to_col):
        span = pl.ds(pl.multiple_of(piece * PIECE, PIECE), PIECE)
        return pltpu.make_async_remote_copy(
            src_ref=low, dst_ref=needed_ref.at[slot, span, :],
            send_sem=low_send.at[to_col], recv_sem=low_recv.at[slot, piece],
            device_id=(to_row, to_col), device_id_type=MESH)

    user, slot = col // factor, col % factor

    @pl.when(row < pieces)
    def _():
        span = pl.ds(pl.multiple_of(row * PIECE, PIECE), PIECE)
        for step in range(1, n_row):
            source = lax.rem(row + step, n_row)
            sum_copy(row, source).wait_recv()
        arrived[row] = part[span, :]
        total = arrived[0]
        for source in range(1, n_row):
            total = total + arrived[source]
        low[...] = total.astype(jnp.bfloat16)
        pulled_ref[span, :] = total
        for to_col in range(n_col):
            mine = jnp.logical_and(user == row, col == to_col)
            pl.when(jnp.logical_not(mine))(lambda: low_copy(row, slot, user, to_col).start())
        for step in range(1, n_row):
            total_copy(row, lax.rem(row + step, n_row)).start()

        @pl.when(user == row)
        def _():
            needed_ref[slot, span, :] = low[...]

    for stream, block, chunk, conds in sends:
        when(*conds)(lambda: move(stream, block, chunk).wait_send())
    for piece in range(pieces):
        pl.when(row != piece)(lambda: sum_copy(piece, row).wait_send())

    @pl.when(row < pieces)
    def _():
        for to_col in range(n_col):
            mine = jnp.logical_and(user == row, col == to_col)
            pl.when(jnp.logical_not(mine))(lambda: low_copy(row, slot, user, to_col).wait_send())
        for step in range(1, n_row):
            total_copy(row, lax.rem(row + step, n_row)).wait_send()

    for piece in range(pieces):
        pl.when(row != piece)(lambda: total_copy(piece, row).wait_recv())
        for at in range(factor):
            mine = jnp.logical_and(row == piece, col == factor * row + at)
            pl.when(jnp.logical_not(mine))(lambda: low_copy(piece, at, row, col).wait_recv())


def operator_kernel(tile, needed_ref, panel_ref, direct_ref, pulled_ref, factor_ref, operator_ref,
                    left, factor, result, factor_sem, result_sem):
    scale = 1.0 / jnp.sqrt(jnp.float32(2.0))
    width = needed_ref.shape[2]
    for at in range(needed_ref.shape[0]):
        left[at * width:(at + 1) * width, :] = needed_ref[at].T

    def store(at):
        span = pl.ds(at * tile, tile)
        return pltpu.make_async_copy(result.at[at], operator_ref.at[:, span], result_sem.at[at])

    tiles = panel_ref.shape[1] // tile
    for at in range(tiles):
        product = jnp.dot(
            left[...], panel_ref[:, at * tile:(at + 1) * tile], preferred_element_type=jnp.float32)
        result[at] = (product * -scale).astype(jnp.bfloat16)
        store(at).start()
        if at == 0:
            factor[...] = (direct_ref[...].astype(jnp.float32) + pulled_ref[...]) * scale
            out = pltpu.make_async_copy(factor, factor_ref, factor_sem)
            out.start()
    for at in range(tiles):
        store(at).wait()
    out.wait()


def body(n_row, n_col, inverse_slab, cot_solved, cot_direct, solved_panel):
    n_states, width = inverse_slab.shape
    columns, depth = cot_solved.shape
    factor = n_col // n_row
    pieces = min(n_row, columns // PIECE)
    chunks = 4 if depth >= 1024 else 1
    hbm = pl.BlockSpec(memory_space=pltpu.HBM)
    vmem = pl.BlockSpec(memory_space=pltpu.VMEM)
    dma = pltpu.SemaphoreType.DMA
    needed, pulled = pl.pallas_call(
        functools.partial(pull_kernel, n_row, n_col, pieces, chunks),
        out_shape=(
            jax.ShapeDtypeStruct((factor, columns, width), jnp.bfloat16),
            jax.ShapeDtypeStruct((columns, width), jnp.float32),
        ),
        in_specs=[hbm, hbm],
        out_specs=(vmem, vmem),
        scratch_shapes=[
            pltpu.VMEM((n_col, chunks, columns, depth // chunks), jnp.bfloat16),
            pltpu.VMEM((n_states, width), jnp.bfloat16),
            pltpu.VMEM((columns, width), jnp.float32),
            pltpu.VMEM((n_row, PIECE, width), jnp.float32),
            pltpu.VMEM((PIECE, width), jnp.bfloat16),
            dma((n_col,)), dma((chunks,)), dma((n_col, chunks)), dma((3, n_col, chunks)),
            dma((pieces,)), dma((n_row,)),
            dma((n_row,)), dma((pieces,)), dma((n_col,)), dma((factor, pieces)),
        ],
        compiler_params=pltpu.CompilerParams(
            collective_id=0, has_side_effects=True, vmem_limit_bytes=48 * 2**20),
        cost_estimate=pl.CostEstimate(
            flops=2 * columns * n_states * width, bytes_accessed=2 * n_states * width, transcendentals=0),
        name="pull",
    )(inverse_slab, pltpu.with_memory_space_constraint(cot_solved, pltpu.HBM))

    panel_width = solved_panel.shape[1]
    tile = min(panel_width, 512)
    tiles = panel_width // tile
    return pl.pallas_call(
        functools.partial(operator_kernel, tile),
        out_shape=(
            jax.ShapeDtypeStruct((columns, width), jnp.float32),
            jax.ShapeDtypeStruct((factor * width, panel_width), jnp.bfloat16),
        ),
        in_specs=[vmem] * 4,
        out_specs=(hbm, hbm),
        scratch_shapes=[
            pltpu.VMEM((factor * width, columns), jnp.bfloat16),
            pltpu.VMEM((columns, width), jnp.float32),
            pltpu.VMEM((tiles, factor * width, tile), jnp.bfloat16),
            dma, dma((tiles,)),
        ],
        compiler_params=pltpu.CompilerParams(vmem_limit_bytes=32 * 2**20),
        cost_estimate=pl.CostEstimate(
            flops=2 * columns * factor * width * panel_width,
            bytes_accessed=2 * factor * width * panel_width, transcendentals=0),
        name="operator",
    )(needed, solved_panel, cot_direct, pulled)


def solution(mesh):
    n_row, n_col = mesh.shape["row"], mesh.shape["col"]
    in_specs = (P("row", "col"), P(None, ("row", "col")), P(None, "col"), P(None, "col"))
    out_specs = (P(None, "col"), P("row", "col"))
    return jax.shard_map(
        functools.partial(body, n_row, n_col),
        mesh=mesh, in_specs=in_specs, out_specs=out_specs, check_vma=False)
```

```python
import functools

import jax
import jax.numpy as jnp
from jax import lax
from jax.experimental import pallas as pl
from jax.experimental.pallas import tpu as pltpu
from jax.sharding import PartitionSpec as P

MESH = pl.DeviceIdType.MESH
PIECE = 16


def when(*conds):
    traced = None
    for cond in conds:
        if cond is not True:
            traced = cond if traced is None else jnp.logical_and(traced, cond)
    if traced is None:
        return lambda body: body()
    return pl.when(traced)


def pull_kernel(n_row, n_col, pieces, chunks,
                inverse_ref, cot_ref, needed_ref, pulled_ref,
                gathered, inverse, part, arrived, low,
                load_sem, own_sem, recv_sem, send_sem, sum_send, sum_recv,
                total_send, total_recv, low_send, low_recv):
    row, col = lax.axis_index("row"), lax.axis_index("col")
    line = n_col // 2
    z, x = col // 2, col % 2
    other = 1 - x
    pair = z * 2 + other
    factor = n_col // n_row
    depth = cot_ref.shape[1]
    span_of = depth // chunks
    balance = line >= 4
    split = max(1, chunks // 4)
    has_down, has_up = z > 0, z < line - 1

    def load_inverse(block):
        span = pl.ds(pl.multiple_of(block * depth, depth), depth)
        return pltpu.make_async_copy(inverse_ref.at[span], inverse.at[span], load_sem.at[block])

    def load_own(chunk):
        return pltpu.make_async_copy(
            cot_ref.at[:, pl.ds(chunk * span_of, span_of)], gathered.at[col, chunk], own_sem.at[chunk])

    for chunk in range(chunks):
        load_own(chunk).start()

    barrier = pltpu.get_barrier_semaphore()

    def greet(to_row, to_col):
        pl.semaphore_signal(barrier, inc=1, device_id=(to_row, to_col), device_id_type=MESH)

    greet(row, pair)
    pl.when(has_down)(lambda: greet(row, col - 2))
    pl.when(has_up)(lambda: greet(row, col + 2))
    for step in range(1, n_row):
        greet(lax.rem(row + step, n_row), col)

    load_inverse(col).start()
    part[...] = jnp.zeros_like(part)
    for chunk in range(chunks):
        load_own(chunk).wait()
    pl.semaphore_wait(barrier, n_row + has_down.astype(jnp.int32) + has_up.astype(jnp.int32))

    UP, DOWN, ACROSS = 0, 1, 2
    target = {UP: col + 2, DOWN: col - 2, ACROSS: pair}

    def move(stream, block, chunk):
        piece = gathered.at[block, chunk]
        return pltpu.make_async_remote_copy(
            src_ref=piece, dst_ref=piece,
            send_sem=send_sem.at[stream, block, chunk], recv_sem=recv_sem.at[block, chunk],
            device_id=(row, target[stream]), device_id_type=MESH)

    def receive(block, chunk, *conds):
        when(*conds)(lambda: move(ACROSS, block, chunk).wait_recv())

    def multiply(block, which=tuple(range(chunks))):
        if which[0] == 0:
            load_inverse(block).wait()
        total = part[...]
        for chunk in which:
            span = pl.ds(pl.multiple_of(block * depth + chunk * span_of, span_of), span_of)
            total += jnp.dot(
                gathered[block, chunk], inverse[span, :], preferred_element_type=jnp.float32)
        part[...] = total

    sends = []

    def send(stream, block, chunk, *conds):
        when(*conds)(lambda: move(stream, block, chunk).start())
        sends.append((stream, block, chunk, conds))

    def across_ok(of_z, chunk):
        if not balance:
            return ()
        if chunk >= split:
            return of_z != 0, of_z != line - 1
        return (jnp.logical_not(jnp.logical_and(z == 1, of_z == 0)),
                jnp.logical_not(jnp.logical_and(z == line - 2, of_z == line - 1)))

    def take_pair(step):
        for at, there in ((z - 1 - step, z - 1 - step >= 0), (z + 1 + step, z + 1 + step < line)):
            block = at * 2 + other

            @pl.when(there)
            def _():
                for chunk in range(chunks):
                    if balance and chunk >= split:
                        passed_on = jnp.logical_and(
                            jnp.logical_or(at == 0, at == line - 1), jnp.logical_and(has_up, has_down))
                        receive(block, chunk, jnp.logical_not(passed_on))
                    else:
                        receive(block, chunk)
                multiply(block)

    bottom, top = other, (line - 1) * 2 + other

    def send_own(chunk):
        send(UP, col, chunk, has_up)
        send(DOWN, col, chunk, has_down)
        send(ACROSS, col, chunk)

    for chunk in range(chunks):
        send_own(chunk)

    def load_step(step):
        for at, there in ((z - 1 - step, z - 1 - step >= 0), (z + 1 + step, z + 1 + step < line)):
            for side in (x, other):
                pl.when(there)(lambda: load_inverse(at * 2 + side).start())

    load_inverse(pair).start()
    load_step(0)
    multiply(col)

    for step in range(line - 1):
        below, above = z - 1 - step, z + 1 + step
        if step >= 1:
            load_step(step)
        for chunk in range(chunks):
            receive(below * 2 + x, chunk, below >= 0)
            send(UP, below * 2 + x, chunk, below >= 0, has_up)
            send(ACROSS, below * 2 + x, chunk, below >= 0, *across_ok(below, chunk))
            receive(above * 2 + x, chunk, above < line)
            send(DOWN, above * 2 + x, chunk, above < line, has_down)
            send(ACROSS, above * 2 + x, chunk, above < line, *across_ok(above, chunk))
        if balance and step >= 1:
            for chunk in range(split, chunks):
                receive(bottom, chunk, z == step)
                send(UP, bottom, chunk, z == step)
                receive(top, chunk, z == line - 1 - step)
                send(DOWN, top, chunk, z == line - 1 - step)
        if step == 0:
            for chunk in range(chunks):
                receive(pair, chunk)
                if balance:
                    send(UP, pair, chunk, z == 0)
                    send(DOWN, pair, chunk, z == line - 1)
        pl.when(below >= 0)(lambda: multiply(below * 2 + x))
        pl.when(above < line)(lambda: multiply(above * 2 + x))
        if step == 0:
            multiply(pair)
        if step >= 2:
            take_pair(step - 2)
    if line >= 3:
        take_pair(line - 3)

    for at, there in ((0, jnp.logical_not(has_up)), (line - 1, jnp.logical_not(has_down))):
        block = at * 2 + other

        @pl.when(there)
        def _():
            for chunk in range(chunks):
                receive(block, chunk)
                multiply(block, (chunk,))

    def sum_copy(piece, source):
        return pltpu.make_async_remote_copy(
            src_ref=part.at[pl.ds(piece * PIECE, PIECE), :], dst_ref=arrived.at[source],
            send_sem=sum_send.at[piece], recv_sem=sum_recv.at[source],
            device_id=(piece, col), device_id_type=MESH)

    for piece in range(pieces):
        pl.when(row != piece)(lambda: sum_copy(piece, row).start())

    def total_copy(piece, to_row):
        span = pl.ds(pl.multiple_of(piece * PIECE, PIECE), PIECE)
        return pltpu.make_async_remote_copy(
            src_ref=pulled_ref.at[span, :], dst_ref=pulled_ref.at[span, :],
            send_sem=total_send.at[to_row], recv_sem=total_recv.at[piece],
            device_id=(to_row, col), device_id_type=MESH)

    def low_copy(piece, slot, to_row, to_col):
        span = pl.ds(pl.multiple_of(piece * PIECE, PIECE), PIECE)
        return pltpu.make_async_remote_copy(
            src_ref=low, dst_ref=needed_ref.at[slot, span, :],
            send_sem=low_send.at[to_col], recv_sem=low_recv.at[slot, piece],
            device_id=(to_row, to_col), device_id_type=MESH)

    user, slot = col // factor, col % factor

    @pl.when(row < pieces)
    def _():
        span = pl.ds(pl.multiple_of(row * PIECE, PIECE), PIECE)
        for step in range(1, n_row):
            source = lax.rem(row + step, n_row)
            sum_copy(row, source).wait_recv()
        arrived[row] = part[span, :]
        total = arrived[0]
        for source in range(1, n_row):
            total = total + arrived[source]
        low[...] = total.astype(jnp.bfloat16)
        pulled_ref[span, :] = total
        for to_col in range(n_col):
            mine = jnp.logical_and(user == row, col == to_col)
            pl.when(jnp.logical_not(mine))(lambda: low_copy(row, slot, user, to_col).start())
        for step in range(1, n_row):
            total_copy(row, lax.rem(row + step, n_row)).start()

        @pl.when(user == row)
        def _():
            needed_ref[slot, span, :] = low[...]

    for stream, block, chunk, conds in sends:
        when(*conds)(lambda: move(stream, block, chunk).wait_send())
    for piece in range(pieces):
        pl.when(row != piece)(lambda: sum_copy(piece, row).wait_send())

    @pl.when(row < pieces)
    def _():
        for to_col in range(n_col):
            mine = jnp.logical_and(user == row, col == to_col)
            pl.when(jnp.logical_not(mine))(lambda: low_copy(row, slot, user, to_col).wait_send())
        for step in range(1, n_row):
            total_copy(row, lax.rem(row + step, n_row)).wait_send()

    for piece in range(pieces):
        pl.when(row != piece)(lambda: total_copy(piece, row).wait_recv())
        for at in range(factor):
            mine = jnp.logical_and(row == piece, col == factor * row + at)
            pl.when(jnp.logical_not(mine))(lambda: low_copy(piece, at, row, col).wait_recv())


def operator_kernel(tile, needed_ref, panel_ref, direct_ref, pulled_ref, factor_ref, operator_ref,
                    left, factor, result, factor_sem, result_sem):
    scale = 1.0 / jnp.sqrt(jnp.float32(2.0))
    width = needed_ref.shape[2]
    for at in range(needed_ref.shape[0]):
        left[at * width:(at + 1) * width, :] = needed_ref[at].T

    def store(at):
        span = pl.ds(at * tile, tile)
        return pltpu.make_async_copy(result.at[at], operator_ref.at[:, span], result_sem.at[at])

    tiles = panel_ref.shape[1] // tile
    for at in range(tiles):
        product = jnp.dot(
            left[...], panel_ref[:, at * tile:(at + 1) * tile], preferred_element_type=jnp.float32)
        result[at] = (product * -scale).astype(jnp.bfloat16)
        store(at).start()
        if at == 0:
            factor[...] = (direct_ref[...].astype(jnp.float32) + pulled_ref[...]) * scale
            out = pltpu.make_async_copy(factor, factor_ref, factor_sem)
            out.start()
    for at in range(tiles):
        store(at).wait()
    out.wait()


def body(n_row, n_col, inverse_slab, cot_solved, cot_direct, solved_panel):
    n_states, width = inverse_slab.shape
    columns, depth = cot_solved.shape
    factor = n_col // n_row
    pieces = min(n_row, columns // PIECE)
    chunks = 4 if depth >= 1024 else 1
    hbm = pl.BlockSpec(memory_space=pltpu.HBM)
    vmem = pl.BlockSpec(memory_space=pltpu.VMEM)
    dma = pltpu.SemaphoreType.DMA
    needed, pulled = pl.pallas_call(
        functools.partial(pull_kernel, n_row, n_col, pieces, chunks),
        out_shape=(
            jax.ShapeDtypeStruct((factor, columns, width), jnp.bfloat16),
            jax.ShapeDtypeStruct((columns, width), jnp.float32),
        ),
        in_specs=[hbm, hbm],
        out_specs=(vmem, vmem),
        scratch_shapes=[
            pltpu.VMEM((n_col, chunks, columns, depth // chunks), jnp.bfloat16),
            pltpu.VMEM((n_states, width), jnp.bfloat16),
            pltpu.VMEM((columns, width), jnp.float32),
            pltpu.VMEM((n_row, PIECE, width), jnp.float32),
            pltpu.VMEM((PIECE, width), jnp.bfloat16),
            dma((n_col,)), dma((chunks,)), dma((n_col, chunks)), dma((3, n_col, chunks)),
            dma((pieces,)), dma((n_row,)),
            dma((n_row,)), dma((pieces,)), dma((n_col,)), dma((factor, pieces)),
        ],
        compiler_params=pltpu.CompilerParams(
            collective_id=0, has_side_effects=True, vmem_limit_bytes=48 * 2**20),
        cost_estimate=pl.CostEstimate(
            flops=2 * columns * n_states * width, bytes_accessed=2 * n_states * width, transcendentals=0),
        name="pull",
    )(inverse_slab, pltpu.with_memory_space_constraint(cot_solved, pltpu.HBM))

    panel_width = solved_panel.shape[1]
    tile = min(panel_width, 512)
    tiles = panel_width // tile
    return pl.pallas_call(
        functools.partial(operator_kernel, tile),
        out_shape=(
            jax.ShapeDtypeStruct((columns, width), jnp.float32),
            jax.ShapeDtypeStruct((factor * width, panel_width), jnp.bfloat16),
        ),
        in_specs=[vmem] * 4,
        out_specs=(hbm, hbm),
        scratch_shapes=[
            pltpu.VMEM((factor * width, columns), jnp.bfloat16),
            pltpu.VMEM((columns, width), jnp.float32),
            pltpu.VMEM((tiles, factor * width, tile), jnp.bfloat16),
            dma, dma((tiles,)),
        ],
        compiler_params=pltpu.CompilerParams(vmem_limit_bytes=32 * 2**20),
        cost_estimate=pl.CostEstimate(
            flops=2 * columns * factor * width * panel_width,
            bytes_accessed=2 * factor * width * panel_width, transcendentals=0),
        name="operator",
    )(needed, solved_panel, cot_direct, pulled)


def solution(mesh):
    n_row, n_col = mesh.shape["row"], mesh.shape["col"]
    in_specs = (P("row", "col"), P(None, ("row", "col")), P(None, "col"), P(None, "col"))
    out_specs = (P(None, "col"), P("row", "col"))
    return jax.shard_map(
        functools.partial(body, n_row, n_col),
        mesh=mesh, in_specs=in_specs, out_specs=out_specs, check_vma=False)
```

```python
import functools

import jax
import jax.numpy as jnp
from jax import lax
from jax.experimental import pallas as pl
from jax.experimental.pallas import tpu as pltpu
from jax.sharding import PartitionSpec as P

MESH = pl.DeviceIdType.MESH
PIECE = 16


def when(*conds):
    traced = None
    for cond in conds:
        if cond is not True:
            traced = cond if traced is None else jnp.logical_and(traced, cond)
    if traced is None:
        return lambda body: body()
    return pl.when(traced)


def pull_kernel(n_row, n_col, pieces, chunks,
                inverse_ref, cot_ref, needed_ref, pulled_ref,
                gathered, inverse, part, arrived, low,
                load_sem, own_sem, recv_sem, send_sem, sum_send, sum_recv,
                total_send, total_recv, low_send, low_recv):
    row, col = lax.axis_index("row"), lax.axis_index("col")
    line = n_col // 2
    z, x = col // 2, col % 2
    other = 1 - x
    pair = z * 2 + other
    factor = n_col // n_row
    depth = cot_ref.shape[1]
    span_of = depth // chunks
    balance = line >= 4
    split = max(1, chunks // 2)
    has_down, has_up = z > 0, z < line - 1

    def load_inverse(block):
        span = pl.ds(pl.multiple_of(block * depth, depth), depth)
        return pltpu.make_async_copy(inverse_ref.at[span], inverse.at[span], load_sem.at[block])

    def load_own(chunk):
        return pltpu.make_async_copy(
            cot_ref.at[:, pl.ds(chunk * span_of, span_of)], gathered.at[col, chunk], own_sem.at[chunk])

    for chunk in range(chunks):
        load_own(chunk).start()

    barrier = pltpu.get_barrier_semaphore()

    def greet(to_row, to_col):
        pl.semaphore_signal(barrier, inc=1, device_id=(to_row, to_col), device_id_type=MESH)

    greet(row, pair)
    pl.when(has_down)(lambda: greet(row, col - 2))
    pl.when(has_up)(lambda: greet(row, col + 2))
    for step in range(1, n_row):
        greet(lax.rem(row + step, n_row), col)

    load_inverse(col).start()
    part[...] = jnp.zeros_like(part)
    for chunk in range(chunks):
        load_own(chunk).wait()
    pl.semaphore_wait(barrier, n_row + has_down.astype(jnp.int32) + has_up.astype(jnp.int32))

    UP, DOWN, ACROSS = 0, 1, 2
    target = {UP: col + 2, DOWN: col - 2, ACROSS: pair}

    def move(stream, block, chunk):
        piece = gathered.at[block, chunk]
        return pltpu.make_async_remote_copy(
            src_ref=piece, dst_ref=piece,
            send_sem=send_sem.at[stream, block, chunk], recv_sem=recv_sem.at[block, chunk],
            device_id=(row, target[stream]), device_id_type=MESH)

    def receive(block, chunk, *conds):
        when(*conds)(lambda: move(ACROSS, block, chunk).wait_recv())

    def multiply(block, which=tuple(range(chunks))):
        if which[0] == 0:
            load_inverse(block).wait()
        total = part[...]
        for chunk in which:
            span = pl.ds(pl.multiple_of(block * depth + chunk * span_of, span_of), span_of)
            total += jnp.dot(
                gathered[block, chunk], inverse[span, :], preferred_element_type=jnp.float32)
        part[...] = total

    sends = []

    def send(stream, block, chunk, *conds):
        when(*conds)(lambda: move(stream, block, chunk).start())
        sends.append((stream, block, chunk, conds))

    def across_ok(of_z, chunk):
        if not balance:
            return ()
        if chunk >= split:
            return of_z != 0, of_z != line - 1
        return (jnp.logical_not(jnp.logical_and(z == 1, of_z == 0)),
                jnp.logical_not(jnp.logical_and(z == line - 2, of_z == line - 1)))

    def take_pair(step):
        for at, there in ((z - 1 - step, z - 1 - step >= 0), (z + 1 + step, z + 1 + step < line)):
            block = at * 2 + other

            @pl.when(there)
            def _():
                for chunk in range(chunks):
                    if balance and chunk >= split:
                        passed_on = jnp.logical_and(
                            jnp.logical_or(at == 0, at == line - 1), jnp.logical_and(has_up, has_down))
                        receive(block, chunk, jnp.logical_not(passed_on))
                    else:
                        receive(block, chunk)
                multiply(block)

    bottom, top = other, (line - 1) * 2 + other

    def send_own(chunk):
        send(UP, col, chunk, has_up)
        send(DOWN, col, chunk, has_down)
        send(ACROSS, col, chunk)

    for chunk in range(chunks):
        send_own(chunk)

    def load_step(step):
        for at, there in ((z - 1 - step, z - 1 - step >= 0), (z + 1 + step, z + 1 + step < line)):
            for side in (x, other):
                pl.when(there)(lambda: load_inverse(at * 2 + side).start())

    load_inverse(pair).start()
    load_step(0)
    multiply(col)

    for step in range(line - 1):
        below, above = z - 1 - step, z + 1 + step
        if step >= 1:
            load_step(step)
        for chunk in range(chunks):
            receive(below * 2 + x, chunk, below >= 0)
            send(UP, below * 2 + x, chunk, below >= 0, has_up)
            send(ACROSS, below * 2 + x, chunk, below >= 0, *across_ok(below, chunk))
            receive(above * 2 + x, chunk, above < line)
            send(DOWN, above * 2 + x, chunk, above < line, has_down)
            send(ACROSS, above * 2 + x, chunk, above < line, *across_ok(above, chunk))
        if balance and step >= 1:
            for chunk in range(split, chunks):
                receive(bottom, chunk, z == step)
                send(UP, bottom, chunk, z == step)
                receive(top, chunk, z == line - 1 - step)
                send(DOWN, top, chunk, z == line - 1 - step)
        if step == 0:
            for chunk in range(chunks):
                receive(pair, chunk)
                if balance:
                    send(UP, pair, chunk, z == 0)
                    send(DOWN, pair, chunk, z == line - 1)
        pl.when(below >= 0)(lambda: multiply(below * 2 + x))
        pl.when(above < line)(lambda: multiply(above * 2 + x))
        if step == 0:
            multiply(pair)
        if step >= 1:
            take_pair(step - 1)

    for at, there in ((0, jnp.logical_not(has_up)), (line - 1, jnp.logical_not(has_down))):
        block = at * 2 + other

        @pl.when(there)
        def _():
            group = max(1, chunks // 4)
            for first in range(0, chunks, group):
                some = tuple(range(first, first + group))
                for chunk in some:
                    receive(block, chunk)
                multiply(block, some)

    def sum_copy(piece, source):
        return pltpu.make_async_remote_copy(
            src_ref=part.at[pl.ds(piece * PIECE, PIECE), :], dst_ref=arrived.at[source],
            send_sem=sum_send.at[piece], recv_sem=sum_recv.at[source],
            device_id=(piece, col), device_id_type=MESH)

    for piece in range(pieces):
        pl.when(row != piece)(lambda: sum_copy(piece, row).start())

    def total_copy(piece, to_row):
        span = pl.ds(pl.multiple_of(piece * PIECE, PIECE), PIECE)
        return pltpu.make_async_remote_copy(
            src_ref=pulled_ref.at[span, :], dst_ref=pulled_ref.at[span, :],
            send_sem=total_send.at[to_row], recv_sem=total_recv.at[piece],
            device_id=(to_row, col), device_id_type=MESH)

    def low_copy(piece, slot, to_row, to_col):
        span = pl.ds(pl.multiple_of(piece * PIECE, PIECE), PIECE)
        return pltpu.make_async_remote_copy(
            src_ref=low, dst_ref=needed_ref.at[slot, span, :],
            send_sem=low_send.at[to_col], recv_sem=low_recv.at[slot, piece],
            device_id=(to_row, to_col), device_id_type=MESH)

    user, slot = col // factor, col % factor

    @pl.when(row < pieces)
    def _():
        span = pl.ds(pl.multiple_of(row * PIECE, PIECE), PIECE)
        for step in range(1, n_row):
            source = lax.rem(row + step, n_row)
            sum_copy(row, source).wait_recv()
        arrived[row] = part[span, :]
        total = arrived[0]
        for source in range(1, n_row):
            total = total + arrived[source]
        low[...] = total.astype(jnp.bfloat16)
        pulled_ref[span, :] = total
        for to_col in range(n_col):
            mine = jnp.logical_and(user == row, col == to_col)
            pl.when(jnp.logical_not(mine))(lambda: low_copy(row, slot, user, to_col).start())
        for step in range(1, n_row):
            total_copy(row, lax.rem(row + step, n_row)).start()

        @pl.when(user == row)
        def _():
            needed_ref[slot, span, :] = low[...]

    for stream, block, chunk, conds in sends:
        when(*conds)(lambda: move(stream, block, chunk).wait_send())
    for piece in range(pieces):
        pl.when(row != piece)(lambda: sum_copy(piece, row).wait_send())

    @pl.when(row < pieces)
    def _():
        for to_col in range(n_col):
            mine = jnp.logical_and(user == row, col == to_col)
            pl.when(jnp.logical_not(mine))(lambda: low_copy(row, slot, user, to_col).wait_send())
        for step in range(1, n_row):
            total_copy(row, lax.rem(row + step, n_row)).wait_send()

    for piece in range(pieces):
        pl.when(row != piece)(lambda: total_copy(piece, row).wait_recv())
        for at in range(factor):
            mine = jnp.logical_and(row == piece, col == factor * row + at)
            pl.when(jnp.logical_not(mine))(lambda: low_copy(piece, at, row, col).wait_recv())


def operator_kernel(tile, needed_ref, panel_ref, direct_ref, pulled_ref, factor_ref, operator_ref,
                    left, factor, result, factor_sem, result_sem):
    scale = 1.0 / jnp.sqrt(jnp.float32(2.0))
    width = needed_ref.shape[2]
    for at in range(needed_ref.shape[0]):
        left[at * width:(at + 1) * width, :] = needed_ref[at].T

    def store(at):
        span = pl.ds(at * tile, tile)
        return pltpu.make_async_copy(result.at[at], operator_ref.at[:, span], result_sem.at[at])

    tiles = panel_ref.shape[1] // tile
    for at in range(tiles):
        product = jnp.dot(
            left[...], panel_ref[:, at * tile:(at + 1) * tile], preferred_element_type=jnp.float32)
        result[at] = (product * -scale).astype(jnp.bfloat16)
        store(at).start()
        if at == 0:
            factor[...] = (direct_ref[...].astype(jnp.float32) + pulled_ref[...]) * scale
            out = pltpu.make_async_copy(factor, factor_ref, factor_sem)
            out.start()
    for at in range(tiles):
        store(at).wait()
    out.wait()


def body(n_row, n_col, inverse_slab, cot_solved, cot_direct, solved_panel):
    n_states, width = inverse_slab.shape
    columns, depth = cot_solved.shape
    factor = n_col // n_row
    pieces = min(n_row, columns // PIECE)
    chunks = 8 if depth >= 1024 else 1
    hbm = pl.BlockSpec(memory_space=pltpu.HBM)
    vmem = pl.BlockSpec(memory_space=pltpu.VMEM)
    dma = pltpu.SemaphoreType.DMA
    needed, pulled = pl.pallas_call(
        functools.partial(pull_kernel, n_row, n_col, pieces, chunks),
        out_shape=(
            jax.ShapeDtypeStruct((factor, columns, width), jnp.bfloat16),
            jax.ShapeDtypeStruct((columns, width), jnp.float32),
        ),
        in_specs=[hbm, hbm],
        out_specs=(vmem, vmem),
        scratch_shapes=[
            pltpu.VMEM((n_col, chunks, columns, depth // chunks), jnp.bfloat16),
            pltpu.VMEM((n_states, width), jnp.bfloat16),
            pltpu.VMEM((columns, width), jnp.float32),
            pltpu.VMEM((n_row, PIECE, width), jnp.float32),
            pltpu.VMEM((PIECE, width), jnp.bfloat16),
            dma((n_col,)), dma((chunks,)), dma((n_col, chunks)), dma((3, n_col, chunks)),
            dma((pieces,)), dma((n_row,)),
            dma((n_row,)), dma((pieces,)), dma((n_col,)), dma((factor, pieces)),
        ],
        compiler_params=pltpu.CompilerParams(
            collective_id=0, has_side_effects=True, vmem_limit_bytes=48 * 2**20),
        cost_estimate=pl.CostEstimate(
            flops=2 * columns * n_states * width, bytes_accessed=2 * n_states * width, transcendentals=0),
        name="pull",
    )(inverse_slab, pltpu.with_memory_space_constraint(cot_solved, pltpu.HBM))

    panel_width = solved_panel.shape[1]
    tile = min(panel_width, 512)
    tiles = panel_width // tile
    return pl.pallas_call(
        functools.partial(operator_kernel, tile),
        out_shape=(
            jax.ShapeDtypeStruct((columns, width), jnp.float32),
            jax.ShapeDtypeStruct((factor * width, panel_width), jnp.bfloat16),
        ),
        in_specs=[vmem] * 4,
        out_specs=(hbm, hbm),
        scratch_shapes=[
            pltpu.VMEM((factor * width, columns), jnp.bfloat16),
            pltpu.VMEM((columns, width), jnp.float32),
            pltpu.VMEM((tiles, factor * width, tile), jnp.bfloat16),
            dma, dma((tiles,)),
        ],
        compiler_params=pltpu.CompilerParams(vmem_limit_bytes=32 * 2**20),
        cost_estimate=pl.CostEstimate(
            flops=2 * columns * factor * width * panel_width,
            bytes_accessed=2 * factor * width * panel_width, transcendentals=0),
        name="operator",
    )(needed, solved_panel, cot_direct, pulled)


def solution(mesh):
    n_row, n_col = mesh.shape["row"], mesh.shape["col"]
    in_specs = (P("row", "col"), P(None, ("row", "col")), P(None, "col"), P(None, "col"))
    out_specs = (P(None, "col"), P("row", "col"))
    return jax.shard_map(
        functools.partial(body, n_row, n_col),
        mesh=mesh, in_specs=in_specs, out_specs=out_specs, check_vma=False)
```
